32 devices in a mesh: dp: 4 (over y, x), member: 2 (over core), expert: 4 (over z).
Axes of the slice: x: 2, y: 2, z: 4, core: 2. Of those that a mesh axis runs over, the one named last changes fastest.
Arguments:
- tokens: bfloat16 [1024, 1280], P(('dp', 'member')), may hold values from -6 to 6
- route_ids: int32 [2, 1024, 1], P(None, ('dp', 'member')), may hold values from 0 to 3; in each aligned block of 128 rows (0 to 127, 128 to 255, ..., all dimensions but the last counted through in order) at most 48 rows name the same one
- router: float32 [2, 1280, 4], replicated, may hold values from -0.15625 to 0.15625
- w_in: bfloat16 [2, 4, 1280, 4608], P('member', 'dp', None, 'expert'), may hold values from -0.15625 to 0.15625
- w_out: bfloat16 [2, 4, 4608, 1280], P('member', 'dp', 'expert'), may hold values from -0.09375 to 0.09375
- out_grad: bfloat16 [2, 1024, 1280], P(None, ('dp', 'member')), may hold values from -6 to 6
Outputs:
- moe_out: bfloat16 [2, 1024, 1280], P(None, ('dp', 'member'))
- token_grad: float32 [1024, 1280], P(('dp', 'member'))
- first_grad: bfloat16 [2, 4, 1280, 4608], P('member', 'dp', None, 'expert')
- second_grad: bfloat16 [2, 4, 4608, 1280], P('member', 'dp', 'expert')
- router_grad: float32 [2, 1280, 4], replicated
The draws below stay inside these ranges and needn't reach their ends.
Inputs may be any that keep to these rules, and one draw needn't show every extreme that they name: `route_ids`: in each aligned block of 128 rows of one member no expert is named by more than 48 rows, and some block names some expert exactly 48 times.
All inputs are finite; a program needn't handle non-finite values.
Results may differ from the reference program's by a relative error of at most 0.022.
Values may be sent and summed in bfloat16 or wider, within the bound.
A program may use at most 64 MiB of HBM per device.

```python
import math
import jax
import jax.numpy as jnp
import numpy as np
from jax import lax

D = 1280
HID = 4608
TOK_DEV = 128
MEMBERS = 2
EXPERTS = 4
TOKENS = 1024
CAP = 48
N_EXPERT = 4


def block_levels(key, shape, cuts, low, top_value):
    level, own = 1.0, jax.random.fold_in(key, 6)
    for position, blocks in cuts:
        steps = jnp.exp(jax.random.uniform(jax.random.fold_in(own, position), (blocks,), jnp.float32, low / len(cuts), top_value / len(cuts)))
        level = level * jnp.repeat(steps, shape[position] // blocks).reshape([-1 if axis == position else 1 for axis in range(len(shape))])
    return level


def shared_out(rng, own, number, rows, amount, top, bound, slope):
    sequence = jax.random.permutation(rng, amount)
    crowded, ordinary = portions_of(amount, rows * top, bound, slope, True), portions_of(amount, rows * top, bound, slope, False)
    places = jnp.arange(amount)

    def named(sizes, rotation):
        used = int((sizes > 0).sum())
        fixed = max(1, used // 4)
        shifted = fixed + (places - fixed + rotation * (used - fixed)) % max(1, amount - fixed)
        return jnp.zeros((amount,), jnp.int32).at[sequence[jnp.where(places < fixed, places, shifted)]].set(jnp.asarray(sizes, jnp.int32))

    sizes = jnp.where(number % 4 == 0, named(crowded, number // 4), named(ordinary, number - number // 4 - 1))
    mixed = jax.random.permutation(jax.random.fold_in(own, 3), amount)
    donor, receiver = mixed[0:amount // 2 * 2:2], mixed[1:amount // 2 * 2:2]
    slack = jnp.minimum(sizes[donor] - 1, bound - sizes[receiver]) // 2
    slack = jnp.where((donor == sequence[0]) | (receiver == sequence[0]) | (sizes[receiver] == 0), 0, jnp.maximum(slack, 0))
    shifted = jax.random.randint(jax.random.fold_in(own, 4), (amount // 2,), 0, 1 << 20) % (slack + 1)
    sizes = sizes.at[donor].add(-shifted).at[receiver].add(shifted)
    labels = jnp.searchsorted(jnp.cumsum(sizes), jnp.arange(rows * top), side="right").astype(jnp.int32)
    grid = labels.reshape(top, rows).T
    grid = grid[jax.random.permutation(jax.random.fold_in(own, 1), rows)]
    rotation = jax.random.randint(jax.random.fold_in(own, 2), (rows, 1), 0, top)
    return jnp.take_along_axis(grid, (jnp.arange(top)[None, :] + rotation) % top, axis=1)


def portions_of(amount, total, bound, skew, full):
    weights = [(1 << 20) // math.isqrt(grade ** skew) + 1 for grade in range(1, amount + 1)]
    largest = bound if full else min(bound, max(-(-total // amount), total * weights[0] // sum(weights)))
    least = 1 if total - largest >= amount - 1 else 0
    given, spare = [largest] + [least] * (amount - 1), total - largest - least * (amount - 1)
    while spare > 0:
        free = [i for i in range(1, amount) if given[i] < largest] or [i for i in range(1, amount) if given[i] < bound]
        pool, remaining = sum([weights[i] for i in free]), spare
        for i in free:
            extra = min(bound - given[i], max(1, remaining * weights[i] // pool), spare)
            given[i] = given[i] + extra
            spare = spare - extra
    return np.array(given)


def scatter_about(key, dims, spread, limit, shards=(), held_as=jnp.bfloat16):
    entries = spread * jax.random.normal(key, dims, jnp.float32)
    if shards:
        entries = entries * block_levels(key, dims, shards, -0.22, 0.18)
    return jnp.clip(entries, -limit, limit).astype(held_as)


def setup_inputs(seed: int = 0) -> dict:
    streams_of = jax.random.split(jax.random.key(seed), 7)
    tokens = scatter_about(streams_of[0], (TOKENS, D), 1.0, 6.0, ((0, 8),))
    route_ids_keys = jax.random.split(jax.random.fold_in(streams_of[1], 1), MEMBERS * TOKENS // TOK_DEV)
    route_ids_turns = jax.random.permutation(jax.random.fold_in(streams_of[1], 3), MEMBERS * TOKENS // TOK_DEV)
    route_ids = jax.vmap(lambda own, number: shared_out(jax.random.fold_in(streams_of[1], 2), own, number, TOK_DEV, EXPERTS, 1, CAP, 2))(route_ids_keys, route_ids_turns).reshape((MEMBERS, TOKENS, 1))
    router = scatter_about(streams_of[2], (MEMBERS, D, EXPERTS), D ** -0.5, 0.15625, (), jnp.float32)
    w_in = scatter_about(streams_of[3], (MEMBERS, EXPERTS, D, HID), D ** -0.5, 0.15625, ((0, 2), (1, 4), (3, 4)))
    w_out = scatter_about(streams_of[4], (MEMBERS, EXPERTS, HID, D), HID ** -0.5, 0.09375, ((0, 2), (1, 4), (2, 4)))
    out_grad = scatter_about(streams_of[5], (MEMBERS, TOKENS, D), 1.0, 6.0, ((1, 8),))
    return dict(tokens=tokens, route_ids=route_ids, router=router, w_in=w_in, w_out=w_out, out_grad=out_grad)


tanh_scale = 0.7978845608028654
cubic_term = 0.044715


def gelu_pair(pre_act):
    inner = tanh_scale * (pre_act + cubic_term * pre_act * pre_act * pre_act)
    tanh_value = jnp.tanh(inner)
    value = 0.5 * pre_act * (1.0 + tanh_value)
    gelu_slope = 0.5 * (1.0 + tanh_value) + 0.5 * pre_act * (1.0 - tanh_value * tanh_value) * tanh_scale * (1.0 + 3.0 * cubic_term * pre_act * pre_act)
    return value, gelu_slope


def slot_rank(expert_ids, experts):
    hot_table = (expert_ids[..., None] == jnp.arange(experts, dtype=jnp.int32)).astype(jnp.int32)
    earlier = jnp.cumsum(hot_table, axis=-2) - hot_table
    return jnp.sum(earlier * hot_table, axis=-1).astype(jnp.int32)


def expert_pass(operands):
    x_rows, g_rows, w_first, w_second = operands
    row_count = x_rows.shape[0]
    pre_act = jnp.dot(x_rows, w_first, preferred_element_type=jnp.float32)
    act_value, gelu_slope = gelu_pair(pre_act)
    activation = act_value.astype(jnp.bfloat16)
    hidden_grad = jnp.dot(g_rows, w_second.T, preferred_element_type=jnp.float32)
    pre_grad = (hidden_grad * gelu_slope).astype(jnp.bfloat16)
    grad_first = jnp.dot(x_rows.T, pre_grad, preferred_element_type=jnp.float32)
    grad_second = jnp.dot(activation.T, g_rows, preferred_element_type=jnp.float32)
    block_width = HID // N_EXPERT
    act_blocks = activation.astype(jnp.float32).reshape(row_count, N_EXPERT, block_width)
    second_blocks = w_second.astype(jnp.float32).reshape(N_EXPERT, block_width, D)
    part_out = jnp.einsum("rjh,jhd->jrd", act_blocks, second_blocks, precision=lax.Precision.HIGHEST).astype(jnp.bfloat16)
    out_rows = jnp.sum(part_out.astype(jnp.float32), axis=0).astype(jnp.bfloat16)
    grad_blocks = pre_grad.astype(jnp.float32).reshape(row_count, N_EXPERT, block_width)
    first_blocks = w_first.astype(jnp.float32).reshape(D, N_EXPERT, block_width)
    part_dx = jnp.einsum("rjh,djh->jrd", grad_blocks, first_blocks, precision=lax.Precision.HIGHEST).astype(jnp.bfloat16)
    dx_rows = jnp.sum(part_dx.astype(jnp.float32), axis=0).astype(jnp.bfloat16)
    return out_rows, dx_rows, grad_first, grad_second


def reference(tokens, route_ids, router, w_in, w_out, out_grad):
    sources = TOKENS // TOK_DEV
    buffer_rows = sources * CAP
    expert_ids = route_ids[:, :, 0]
    slot_rows = slot_rank(expert_ids.reshape(MEMBERS, sources, TOK_DEV), EXPERTS).reshape(MEMBERS, TOKENS)
    block_index = (jnp.arange(TOKENS, dtype=jnp.int32) // TOK_DEV).astype(jnp.int32)
    tokens_f = tokens.astype(jnp.float32)
    hot_table = (expert_ids[..., None] == jnp.arange(EXPERTS, dtype=jnp.int32)).astype(jnp.float32)
    logits = jnp.einsum("td,mde->mte", tokens_f, router, precision=lax.Precision.HIGHEST)
    gate_value = jax.nn.sigmoid(jnp.sum(logits * hot_table, axis=-1))
    scaled = (gate_value[..., None] * out_grad.astype(jnp.float32)).astype(jnp.bfloat16)
    token_grad = jnp.zeros((TOKENS, D), jnp.float32)
    moe_list = []
    first_list = []
    second_list = []
    router_list = []
    for member in range(MEMBERS):
        buffer_index = (expert_ids[member] * buffer_rows + block_index * CAP + slot_rows[member]).astype(jnp.int32)
        x_rows = jnp.zeros((EXPERTS * buffer_rows, D), jnp.bfloat16).at[buffer_index].set(tokens).reshape(EXPERTS, buffer_rows, D)
        g_rows = jnp.zeros((EXPERTS * buffer_rows, D), jnp.bfloat16).at[buffer_index].set(scaled[member]).reshape(EXPERTS, buffer_rows, D)
        out_rows, dx_rows, grad_first, grad_second = lax.map(expert_pass, (x_rows, g_rows, w_in[member], w_out[member]))
        expert_output = out_rows.reshape(EXPERTS * buffer_rows, D)[buffer_index]
        expert_dx = dx_rows.reshape(EXPERTS * buffer_rows, D)[buffer_index]
        moe_list.append((gate_value[member][:, None] * expert_output.astype(jnp.float32)).astype(jnp.bfloat16))
        gate_grad = jnp.sum(out_grad[member].astype(jnp.float32) * expert_output.astype(jnp.float32), axis=-1)
        logit_grad = gate_grad * gate_value[member] * (1.0 - gate_value[member])
        weighted = hot_table[member] * logit_grad[:, None]
        router_list.append(jnp.dot(tokens_f.T, weighted, precision=lax.Precision.HIGHEST))
        token_grad = token_grad + expert_dx.astype(jnp.float32) + jnp.dot(weighted, router[member].T, precision=lax.Precision.HIGHEST)
        first_list.append(grad_first.astype(jnp.bfloat16))
        second_list.append(grad_second.astype(jnp.bfloat16))
    return (jnp.stack(moe_list), token_grad, jnp.stack(first_list), jnp.stack(second_list), jnp.stack(router_list))
```

```python
import functools

import jax
import jax.numpy as jnp
from jax import lax
from jax.experimental import pallas as pl
from jax.experimental.pallas import tpu as pltpu
from jax.sharding import PartitionSpec as P

MESH = pl.DeviceIdType.MESH
tanh_scale = 0.7978845608028654
cubic_term = 0.044715


def gelu_pair(pre_act):
    square = pre_act * pre_act
    tanh_value = jnp.tanh(tanh_scale * (pre_act + cubic_term * square * pre_act))
    half = 0.5 * (1.0 + tanh_value)
    slope = half + 0.5 * pre_act * (1.0 - tanh_value * tanh_value) * tanh_scale * (
        1.0 + 3.0 * cubic_term * square
    )
    return pre_act * half, slope


def slot_rank(expert_ids, experts):
    hot_table = (expert_ids[..., None] == jnp.arange(experts, dtype=jnp.int32)).astype(jnp.int32)
    earlier = jnp.cumsum(hot_table, axis=-2) - hot_table
    return jnp.sum(earlier * hot_table, axis=-1)


def dot(a, b, ca, cb, precision=None):
    return lax.dot_general(
        a, b, (((ca,), (cb,)), ((), ())), precision=precision, preferred_element_type=jnp.float32
    )


def tile_of(size, wanted):
    while size % wanted:
        wanted -= 128
    return wanted


def layer_kernel(
    cfg,
    x_send, g_send, w1_hbm, w2_hbm, unperm, tokens, out_grad, hot_rows, gate_slope,
    out_tot, dx_tot, first_hbm, second_hbm, router_all,
    w1, w2, xr, gr, act, slope, pg, po, pd, ro, rd, first, second,
    own, red, xch, res, router_part, router_z, router_sum,
    load_sem, x_ss, x_rs, g_ss, g_rs, o_ss, o_rs, d_ss, d_rs,
    red_ss, red_rs, xch_ss, xch_rs, res_ss, res_rs, rz_ss, rz_rs, rp_ss, rp_rs,
):
    dp, members, zn, cap, toks, chunk = cfg
    peers = dp * members
    me_dp, me_m, me_z = lax.axis_index("dp"), lax.axis_index("member"), lax.axis_index("expert")
    me = me_dp * members + me_m
    width = x_send.shape[-1]
    hidden = w1.shape[1]
    rows = peers * cap

    def plane(index):
        return {"dp": index // members, "member": index % members}

    def loop(count, body):
        lax.fori_loop(0, count, lambda i, c: (body(i), c)[1], 0)

    barrier = pltpu.get_barrier_semaphore()

    def greet_plane(i):
        pl.semaphore_signal(barrier, inc=1, device_id=plane((me + 1 + i) % peers), device_id_type=MESH)

    def greet_z(i):
        pl.semaphore_signal(
            barrier, inc=1, device_id={"expert": (me_z + 1 + i) % zn}, device_id_type=MESH
        )

    loop(peers - 1, greet_plane)
    loop(zn - 1, greet_z)
    load1 = pltpu.make_async_copy(w1_hbm, w1, load_sem.at[0])
    load2 = pltpu.make_async_copy(w2_hbm, w2, load_sem.at[1])
    load1.start()
    load2.start()
    pl.semaphore_wait(barrier, peers + zn - 2)

    def exchange(source, target, send_sem, recv_sem, slot, own_sem):
        def remote(peer):
            return pltpu.make_async_remote_copy(
                src_ref=source.at[peer],
                dst_ref=target.at[slot(me)],
                send_sem=send_sem.at[peer],
                recv_sem=recv_sem.at[me],
                device_id=plane(peer),
                device_id_type=MESH,
            )

        mine = pltpu.make_async_copy(source.at[me], target.at[slot(me)], own_sem)
        mine.start()
        loop(peers - 1, lambda i: remote((me + 1 + i) % peers).start())

        def wait_recv():
            mine.wait()

            def one(i):
                peer = (me + 1 + i) % peers
                pltpu.make_async_remote_copy(
                    src_ref=source.at[peer],
                    dst_ref=target.at[slot(peer)],
                    send_sem=send_sem.at[peer],
                    recv_sem=recv_sem.at[peer],
                    device_id=plane(peer),
                    device_id_type=MESH,
                ).wait_recv()

            loop(peers - 1, one)

        def wait_send():
            loop(peers - 1, lambda i: remote((me + 1 + i) % peers).wait_send())

        return wait_recv, wait_send

    by_source = lambda d: d
    by_member = lambda d: (d % members) * dp + d // members
    x_recv, x_sent = exchange(x_send, xr, x_ss, x_rs, by_source, load_sem.at[2])
    g_recv, g_sent = exchange(g_send, gr, g_ss, g_rs, by_source, load_sem.at[3])

    th = tile_of(hidden, 384)
    td = tile_of(width, 256)
    load1.wait()
    x_recv()

    def first_layer(j):
        cols = pl.ds(pl.multiple_of(j * th, 128), th)
        value, grad = gelu_pair(dot(xr[...].reshape(rows, width), w1[:, cols], 1, 0))
        act[:, cols] = value.astype(jnp.bfloat16)
        slope[:, cols] = grad

    loop(hidden // th, first_layer)
    load2.wait()

    def out_part(j):
        cols = pl.ds(pl.multiple_of(j * td, 128), td)
        part = dot(act[...], w2[:, cols], 1, 0).astype(jnp.bfloat16)
        po[:, :, cols] = part.reshape(peers, cap, td)

    loop(width // td, out_part)
    o_recv, o_sent = exchange(po, ro, o_ss, o_rs, by_member, load_sem.at[4])

    g_recv()

    def hidden_grad(j):
        cols = pl.ds(pl.multiple_of(j * th, 128), th)
        value = dot(gr[...].reshape(rows, width), w2[cols, :], 1, 1) * slope[:, cols]
        pg[:, cols] = value.astype(jnp.bfloat16)

    loop(hidden // th, hidden_grad)

    def dx_part(j):
        cols = pl.ds(pl.multiple_of(j * td, 128), td)
        part = dot(pg[...], w1[cols, :], 1, 1).astype(jnp.bfloat16)
        pd[:, :, cols] = part.reshape(peers, cap, td)

    loop(width // td, dx_part)
    d_recv, d_sent = exchange(pd, rd, d_ss, d_rs, by_member, load_sem.at[5])

    def weight_grads(j):
        cols = pl.ds(pl.multiple_of(j * td, 128), td)
        second[:, cols] = dot(act[...], gr[:, :, cols].reshape(rows, td), 0, 0).astype(jnp.bfloat16)
        first[cols, :] = dot(xr[:, :, cols].reshape(rows, td), pg[...], 0, 0).astype(jnp.bfloat16)

    loop(width // td, weight_grads)
    store1 = pltpu.make_async_copy(first, first_hbm, load_sem.at[0])
    store2 = pltpu.make_async_copy(second, second_hbm, load_sem.at[1])
    store1.start()
    store2.start()

    o_recv()
    router_part[...] = jnp.zeros_like(router_part)
    for m in range(members):
        part = dot(unperm[m], ro[m * dp : (m + 1) * dp].reshape(dp * cap, width), 1, 0)
        own[m * toks : (m + 1) * toks, :] = part.astype(jnp.bfloat16)
        gate_grad = jnp.sum(out_grad[m].astype(jnp.float32) * part, axis=-1, keepdims=True)
        weighted = tokens[...].astype(jnp.float32) * (gate_grad * gate_slope[m])
        router_part[...] += dot(hot_rows[m], weighted, 1, 0, lax.Precision.HIGHEST)

    def router_copy(z_to, z_from):
        return pltpu.make_async_remote_copy(
            src_ref=router_part,
            dst_ref=router_z.at[z_from],
            send_sem=rz_ss.at[z_to],
            recv_sem=rz_rs.at[z_from],
            device_id={"expert": z_to},
            device_id_type=MESH,
        )

    loop(zn - 1, lambda i: router_copy((me_z + 1 + i) % zn, me_z).start())
    router_z[me_z] = router_part[...]

    router_sends = []

    def finish_dx_and_router():
        d_recv()
        total = jnp.zeros((toks, width), jnp.float32)
        for m in range(members):
            total += dot(unperm[m], rd[m * dp : (m + 1) * dp].reshape(dp * cap, width), 1, 0)
        own[members * toks : (members + 1) * toks, :] = total.astype(jnp.bfloat16)
        loop(zn - 1, lambda i: router_copy((me_z + 1 + i) % zn, (me_z + 1 + i) % zn).wait_recv())
        router_sum[...] = jnp.sum(router_z[...], axis=0)
        loop(peers - 1, lambda i: router_plane((me + 1 + i) % peers, me).start())
        pltpu.make_async_copy(router_sum, router_all.at[me], load_sem.at[6]).start()

    def router_plane(to, slot):
        return pltpu.make_async_remote_copy(
            src_ref=router_sum,
            dst_ref=router_all.at[slot],
            send_sem=rp_ss.at[to],
            recv_sem=rp_rs.at[slot],
            device_id=plane(to),
            device_id_type=MESH,
        )

    mid = zn // 2 - 1
    left = me_z < zn // 2
    pos = jnp.where(left, me_z, zn - 1 - me_z)
    inner = jnp.where(left, me_z + 1, me_z - 1)
    outer = jnp.where(left, me_z - 1, me_z + 1)
    total_rows = (members + 1) * toks
    chunks = total_rows // chunk
    dx_chunk = members * toks // chunk

    def piece(k):
        return pl.ds(pl.multiple_of(k * chunk, chunk), chunk)

    def line(source, target, send_sem, recv_sem, k, z_to):
        return pltpu.make_async_remote_copy(
            src_ref=source.at[piece(k)],
            dst_ref=target.at[piece(k)],
            send_sem=send_sem.at[k],
            recv_sem=recv_sem.at[k],
            device_id={"expert": z_to},
            device_id_type=MESH,
        )

    def step(t):
        ka = t - pos
        kb = t - (2 * mid + 1 - pos)

        @pl.when((kb >= 0) & (kb < chunks))
        def _():
            @pl.when(pos == mid)
            def _():
                line(own, xch, xch_ss, xch_rs, kb, inner).wait()
                res[piece(kb), :] = (
                    own[piece(kb), :].astype(jnp.float32) + xch[piece(kb), :].astype(jnp.float32)
                ).astype(jnp.bfloat16)

            @pl.when(pos < mid)
            def _():
                line(res, res, res_ss, res_rs, kb, inner).wait_recv()

            @pl.when(pos > 0)
            def _():
                line(res, res, res_ss, res_rs, kb, outer).start()

        @pl.when(ka == dx_chunk)
        def _():
            finish_dx_and_router()

        @pl.when((ka >= 0) & (ka < chunks))
        def _():
            @pl.when(pos > 0)
            def _():
                line(own, red, red_ss, red_rs, ka, outer).wait_recv()
                own[piece(ka), :] = (
                    own[piece(ka), :].astype(jnp.float32) + red[piece(ka), :].astype(jnp.float32)
                ).astype(jnp.bfloat16)

            @pl.when(pos < mid)
            def _():
                line(own, red, red_ss, red_rs, ka, inner).start()

            @pl.when(pos == mid)
            def _():
                line(own, xch, xch_ss, xch_rs, ka, inner).start()

    loop(chunks + 2 * mid + 1, step)

    def drain(k):
        @pl.when(pos < mid)
        def _():
            line(own, red, red_ss, red_rs, k, inner).wait_send()

        @pl.when(pos > 0)
        def _():
            line(res, res, res_ss, res_rs, k, outer).wait_send()

    out_tot[...] = res[: members * toks, :]
    dx_tot[...] = res[members * toks :, :]
    loop(chunks, drain)
    x_sent()
    g_sent()
    o_sent()
    d_sent()
    store1.wait()
    store2.wait()
    loop(zn - 1, lambda i: router_copy((me_z + 1 + i) % zn, me_z).wait_send())
    loop(peers - 1, lambda i: router_plane((me + 1 + i) % peers, me).wait_send())
    loop(peers - 1, lambda i: router_plane((me + 1 + i) % peers, (me + 1 + i) % peers).wait_recv())
    pltpu.make_async_copy(router_sum, router_all.at[me], load_sem.at[6]).wait()


def shards(tokens, route_ids, router, w_in, w_out, out_grad):
    members, toks = route_ids.shape[:2]
    experts, width = router.shape[2], tokens.shape[1]
    dp, zn = lax.axis_size("dp"), lax.axis_size("expert")
    peers = dp * members
    hidden = w_in.shape[3]
    capacity = max(2, 3 * toks // (2 * experts))
    cap = -(-capacity // 16) * 16
    rows = peers * cap
    chunk = 32

    expert_ids = route_ids[:, :, 0]
    slots = slot_rank(expert_ids, experts)
    expert_range = jnp.arange(experts, dtype=jnp.int32)
    hot = expert_ids[..., None] == expert_range
    hot_f = hot.astype(jnp.float32)
    tokens_f = tokens.astype(jnp.float32)
    logits = jnp.einsum("td,mde->mte", tokens_f, router, precision=lax.Precision.HIGHEST)
    gate = jax.nn.sigmoid(jnp.sum(logits * hot_f, axis=-1))
    scaled = (gate[..., None] * out_grad.astype(jnp.float32)).astype(jnp.bfloat16)
    gate_slope = (gate * (1.0 - gate))[..., None]

    place = expert_ids * cap + slots
    unperm = (place[..., None] == jnp.arange(experts * cap, dtype=jnp.int32)).astype(jnp.bfloat16)
    member_range = jnp.arange(members, dtype=jnp.int32)[:, None]
    send_place = ((expert_ids * members + member_range) * cap + slots).reshape(1, -1)
    pick = (jnp.arange(rows, dtype=jnp.int32)[:, None] == send_place).astype(jnp.bfloat16)
    token_pick = (
        jnp.sum(pick.reshape(rows, members, toks).astype(jnp.float32), axis=1)
    ).astype(jnp.bfloat16)
    x_send = jnp.dot(token_pick, tokens, preferred_element_type=jnp.bfloat16)
    g_send = jnp.dot(pick, scaled.reshape(-1, width), preferred_element_type=jnp.bfloat16)
    hot_rows = (
        (member_range[:, :, None] == member_range[None, :, :])[..., None]
        & jnp.swapaxes(hot, 1, 2)[:, None]
    ).astype(jnp.float32).reshape(members, members * experts, toks)

    bf, f32 = jnp.bfloat16, jnp.float32
    vmem, anywhere = pl.BlockSpec(memory_space=pltpu.VMEM), pl.BlockSpec(memory_space=pl.ANY)
    total_rows = (members + 1) * toks
    chunks = total_rows // chunk
    dma = pltpu.SemaphoreType.DMA
    block = pltpu.VMEM((peers, cap, width), bf)
    line = pltpu.VMEM((total_rows, width), bf)
    router_shape = (members * experts, width)
    out_tot, dx_tot, first, second, router_all = pl.pallas_call(
        functools.partial(layer_kernel, (dp, members, zn, cap, toks, chunk)),
        out_shape=(
            jax.ShapeDtypeStruct((members * toks, width), bf),
            jax.ShapeDtypeStruct((toks, width), bf),
            jax.ShapeDtypeStruct((width, hidden), bf),
            jax.ShapeDtypeStruct((hidden, width), bf),
            jax.ShapeDtypeStruct((peers,) + router_shape, f32),
        ),
        in_specs=[vmem, vmem, anywhere, anywhere] + [vmem] * 5,
        out_specs=(vmem, vmem, anywhere, anywhere, anywhere),
        scratch_shapes=[
            pltpu.VMEM((width, hidden), bf),
            pltpu.VMEM((hidden, width), bf),
            block,
            block,
            pltpu.VMEM((rows, hidden), bf),
            pltpu.VMEM((rows, hidden), f32),
            pltpu.VMEM((rows, hidden), bf),
            block,
            block,
            block,
            block,
            pltpu.VMEM((width, hidden), bf),
            pltpu.VMEM((hidden, width), bf),
            line,
            line,
            line,
            line,
            pltpu.VMEM(router_shape, f32),
            pltpu.VMEM((zn,) + router_shape, f32),
            pltpu.VMEM(router_shape, f32),
            dma((7,)),
        ]
        + [dma((peers,))] * 8
        + [dma((chunks,))] * 6
        + [dma((zn,))] * 2
        + [dma((peers,))] * 2,
        compiler_params=pltpu.CompilerParams(
            collective_id=0, has_side_effects=True, vmem_limit_bytes=60 * 1024 * 1024
        ),
        cost_estimate=pl.CostEstimate(
            flops=12 * rows * width * hidden,
            bytes_accessed=8 * width * hidden,
            transcendentals=rows * hidden,
        ),
    )(
        x_send.reshape(peers, cap, width),
        g_send.reshape(peers, cap, width),
        w_in[0, 0],
        w_out[0, 0],
        unperm,
        tokens,
        out_grad,
        hot_rows,
        gate_slope,
    )

    output_f = out_tot.reshape(members, toks, width).astype(f32)
    moe_out = (gate[..., None] * output_f).astype(bf)
    gate_grad = jnp.sum(out_grad.astype(f32) * output_f, axis=-1)
    weighted = hot_f * (gate_grad[..., None] * gate_slope)
    router_term = jnp.einsum("mte,mde->td", weighted, router, precision=lax.Precision.HIGHEST)
    token_grad = router_term + dx_tot.astype(f32)
    router_grad = jnp.swapaxes(
        jnp.sum(router_all, axis=0).reshape(members, experts, width), 1, 2
    )
    return (moe_out, token_grad, first[None, None], second[None, None], router_grad)


def solution(mesh):
    in_specs = (
        P(("dp", "member"), None),
        P(None, ("dp", "member"), None),
        P(),
        P("member", "dp", None, "expert"),
        P("member", "dp", "expert", None),
        P(None, ("dp", "member"), None),
    )
    out_specs = (
        P(None, ("dp", "member"), None),
        P(("dp", "member"), None),
        P("member", "dp", None, "expert"),
        P("member", "dp", "expert", None),
        P(),
    )
    return jax.shard_map(shards, mesh=mesh, in_specs=in_specs, out_specs=out_specs, check_vma=False)
```

```python
import functools

import jax
import jax.numpy as jnp
from jax import lax
from jax.experimental import pallas as pl
from jax.experimental.pallas import tpu as pltpu
from jax.sharding import PartitionSpec as P

MESH = pl.DeviceIdType.MESH
tanh_scale = 0.7978845608028654
cubic_term = 0.044715


def gelu_pair(pre_act):
    square = pre_act * pre_act
    tanh_value = jnp.tanh(tanh_scale * (pre_act + cubic_term * square * pre_act))
    half = 0.5 * (1.0 + tanh_value)
    slope = half + 0.5 * pre_act * (1.0 - tanh_value * tanh_value) * tanh_scale * (
        1.0 + 3.0 * cubic_term * square
    )
    return pre_act * half, slope


def slot_rank(expert_ids, experts):
    hot_table = (expert_ids[..., None] == jnp.arange(experts, dtype=jnp.int32)).astype(jnp.int32)
    earlier = jnp.cumsum(hot_table, axis=-2) - hot_table
    return jnp.sum(earlier * hot_table, axis=-1)


def dot(a, b, ca, cb, precision=None):
    return lax.dot_general(
        a, b, (((ca,), (cb,)), ((), ())), precision=precision, preferred_element_type=jnp.float32
    )


def tile_of(size, wanted):
    while size % wanted:
        wanted -= 128
    return wanted


def layer_kernel(
    cfg,
    row_place, col_place, row_ids, col_ids, tokens, out_grad, router_t, w1_hbm, w2_hbm,
    moe_out, token_grad, first_hbm, second_hbm, router_all,
    x_send, g_send, picks, unperm, picked_router, gates, gate_grads,
    w1, w2, xr, gr, act, slope, pg, po, pd, ro, rd, first, second,
    own, red, xch, res, router_part, router_z, router_sum,
    load_sem, x_ss, x_rs, g_ss, g_rs, xf_ss, xf_rs, gf_ss, gf_rs, o_ss, o_rs, d_ss, d_rs,
    red_ss, red_rs, xch_ss, xch_rs, res_ss, res_rs, rz_ss, rz_rs, rp_ss, rp_rs,
):
    dp, members, zn, cap, toks, chunk = cfg
    peers = dp * members
    me_dp, me_m, me_z = lax.axis_index("dp"), lax.axis_index("member"), lax.axis_index("expert")
    me = me_dp * members + me_m
    width = x_send.shape[-1]
    half = width // 2
    hidden = w1.shape[1]
    rows = peers * cap
    experts = router_t.shape[1]
    bf, f32 = jnp.bfloat16, jnp.float32

    def plane(index):
        return {"dp": index // members, "member": index % members}

    def loop(count, body):
        lax.fori_loop(0, count, lambda i, c: (body(i), c)[1], 0)

    def each_peer(body):
        loop(peers - 1, lambda i: body((me + 1 + i) % peers))

    def each_z(body):
        loop(zn - 1, lambda i: body((me_z + 1 + i) % zn))

    def remote(source, target, send_sem, recv_sem, where):
        return pltpu.make_async_remote_copy(
            src_ref=source,
            dst_ref=target,
            send_sem=send_sem,
            recv_sem=recv_sem,
            device_id=where,
            device_id_type=MESH,
        )

    barrier = pltpu.get_barrier_semaphore()
    each_peer(
        lambda p: pl.semaphore_signal(barrier, inc=1, device_id=plane(p), device_id_type=MESH)
    )
    each_z(
        lambda z: pl.semaphore_signal(barrier, inc=1, device_id={"expert": z}, device_id_type=MESH)
    )
    load1 = pltpu.make_async_copy(w1_hbm, w1, load_sem.at[0])
    load2 = pltpu.make_async_copy(w2_hbm, w2, load_sem.at[1])
    load1.start()
    load2.start()

    relay = cap % 48 == 0
    third = cap // 3
    parity = me_z % 2
    partner = me_z + 1 - 2 * parity
    if relay:
        sent = pl.ds(pl.multiple_of(parity * third, 16), 2 * third)
        handed = pl.ds(pl.multiple_of(parity * 2 * third, 16), third)
        taken = pl.ds(pl.multiple_of((1 - parity) * 2 * third, 16), third)
    else:
        sent = pl.ds(0, cap)

    def dispatch(source, target, send_sem, recv_sem, relay_ss, relay_rs, own_sem):
        def send(peer, slot):
            return remote(
                source.at[peer, sent], target.at[slot, sent], send_sem.at[peer], recv_sem.at[slot], plane(peer)
            )

        def hand(peer, part):
            return remote(
                target.at[peer, part],
                target.at[peer, part],
                relay_ss.at[peer],
                relay_rs.at[peer],
                {"expert": partner},
            )

        mine = pltpu.make_async_copy(source.at[me], target.at[me], own_sem)

        def start():
            each_peer(lambda p: send(p, me).start())
            mine.start()

        def receive():
            def one(p):
                send(p, p).wait_recv()
                if relay:
                    hand(p, handed).start()

            each_peer(one)
            if relay:
                each_peer(lambda p: hand(p, taken).wait_recv())
            mine.wait()

        def finish():
            each_peer(lambda p: send(p, me).wait_send())
            if relay:
                each_peer(lambda p: hand(p, handed).wait_send())

        return start, receive, finish

    x_start, x_receive, x_finish = dispatch(x_send, xr, x_ss, x_rs, xf_ss, xf_rs, load_sem.at[2])
    g_start, g_receive, g_finish = dispatch(g_send, gr, g_ss, g_rs, gf_ss, gf_rs, load_sem.at[3])

    th = tile_of(hidden, 384)
    td = tile_of(width, 256)

    row_index = lax.broadcasted_iota(jnp.int32, (rows, toks), 0)
    for m in range(members):
        picks[m] = (row_index == row_place[m]).astype(f32).astype(bf)

    def pack_tokens(j):
        cols = pl.ds(pl.multiple_of(j * td, 128), td)
        value = sum(dot(picks[m], tokens[:, cols], 1, 0) for m in range(members))
        x_send[:, :, cols] = value.astype(bf).reshape(peers, cap, td)

    loop(width // td, pack_tokens)
    pl.semaphore_wait(barrier, peers + zn - 2)
    x_start()

    hot_index = lax.broadcasted_iota(jnp.int32, (toks, experts), 1)
    tokens_f = tokens[...].astype(f32)
    for m in range(members):
        hot = (hot_index == col_ids[m]).astype(f32)
        picked_router[m] = dot(hot, router_t[m], 1, 0, lax.Precision.HIGHEST)
        logit = jnp.sum(tokens_f * picked_router[m], axis=-1, keepdims=True)
        gates[m] = 1.0 / (1.0 + jnp.exp(-logit))

    def pack_grads(j):
        cols = pl.ds(pl.multiple_of(j * td, 128), td)
        value = sum(
            dot(picks[m], (gates[m] * out_grad[m, :, cols].astype(f32)).astype(bf), 1, 0)
            for m in range(members)
        )
        g_send[:, :, cols] = value.astype(bf).reshape(peers, cap, td)

    loop(width // td, pack_grads)
    g_start()
    place_index = lax.broadcasted_iota(jnp.int32, (toks, dp * cap), 1)
    for m in range(members):
        unperm[m] = (place_index == col_place[m]).astype(f32).astype(bf)

    load1.wait()
    x_receive()

    def first_layer(j):
        cols = pl.ds(pl.multiple_of(j * th, 128), th)
        value, grad = gelu_pair(dot(xr[...].reshape(rows, width), w1[:, cols], 1, 0))
        act[:, cols] = value.astype(bf)
        slope[:, cols] = grad

    loop(hidden // th, first_layer)
    load2.wait()

    by_member = lambda d: (d % members) * dp + d // members

    def give_back(source, target, send_sem, recv_sem, h, own_sem):
        def send(peer, sender):
            return remote(
                source.at[h, peer],
                target.at[h, by_member(sender)],
                send_sem.at[h, peer],
                recv_sem.at[h, sender],
                plane(peer),
            )

        mine = pltpu.make_async_copy(source.at[h, me], target.at[h, by_member(me)], own_sem)

        def start():
            each_peer(lambda p: send(p, me).start())
            mine.start()

        def receive():
            each_peer(lambda p: send(p, p).wait_recv())
            mine.wait()

        return start, receive, lambda: each_peer(lambda p: send(p, me).wait_send())

    outs = [give_back(po, ro, o_ss, o_rs, h, load_sem.at[4 + h]) for h in range(2)]
    dxs = [give_back(pd, rd, d_ss, d_rs, h, load_sem.at[6 + h]) for h in range(2)]

    for h in range(2):
        part = dot(act[...], w2[:, h * half : (h + 1) * half], 1, 0).astype(bf)
        po[h] = part.reshape(peers, cap, half)
        outs[h][0]()

    g_receive()

    def hidden_grad(j):
        cols = pl.ds(pl.multiple_of(j * th, 128), th)
        value = dot(gr[...].reshape(rows, width), w2[cols, :], 1, 1) * slope[:, cols]
        pg[:, cols] = value.astype(bf)

    loop(hidden // th, hidden_grad)
    for h in range(2):
        part = dot(pg[...], w1[h * half : (h + 1) * half, :], 1, 1).astype(bf)
        pd[h] = part.reshape(peers, cap, half)
        dxs[h][0]()

    mid = zn // 2 - 1
    left = me_z < zn // 2
    pos = jnp.where(left, me_z, zn - 1 - me_z)
    inner = jnp.where(left, me_z + 1, me_z - 1)
    outer = jnp.where(left, me_z - 1, me_z + 1)
    out_chunks = members * toks // chunk
    dx_chunks = toks // chunk
    chunks = 2 * (out_chunks + dx_chunks)
    per_member = toks // chunk
    lag = 2
    store1 = pltpu.make_async_copy(first, first_hbm, load_sem.at[0])
    store2 = pltpu.make_async_copy(second, second_hbm, load_sem.at[1])

    def router_copy(z_to, z_from):
        return remote(
            router_part, router_z.at[z_from], rz_ss.at[z_to], rz_rs.at[z_from], {"expert": z_to}
        )

    def router_plane(to, slot):
        return remote(router_sum, router_all.at[slot], rp_ss.at[to], rp_rs.at[slot], plane(to))

    router_mine = pltpu.make_async_copy(router_sum, router_all.at[me], load_sem.at[8])

    def second_grads(j):
        cols = pl.ds(pl.multiple_of(j * td, 128), td)
        second[:, cols] = dot(act[...], gr[:, :, cols].reshape(rows, td), 0, 0).astype(bf)

    def first_grads(j):
        cols = pl.ds(pl.multiple_of(j * td, 128), td)
        first[cols, :] = dot(xr[:, :, cols].reshape(rows, td), pg[...], 0, 0).astype(bf)

    def take_out(h):
        outs[h][1]()
        for m in range(members):
            part = dot(unperm[m], ro[h, m * dp : (m + 1) * dp].reshape(dp * cap, half), 1, 0)
            base = h * out_chunks + m * per_member
            own[base : base + per_member] = part.astype(bf).reshape(per_member, chunk, half)
            grad = out_grad[m, :, h * half : (h + 1) * half].astype(f32)
            partial = jnp.sum(grad * part, axis=-1, keepdims=True)
            gate_grads[m] = partial if h == 0 else gate_grads[m] + partial

    def send_router():
        total = jnp.zeros(router_part.shape, f32)
        hot_row = lax.broadcasted_iota(jnp.int32, (members * experts, toks), 0)
        for m in range(members):
            hot = (hot_row == row_ids[m] + m * experts).astype(f32)
            weight = gate_grads[m] * gates[m] * (1.0 - gates[m])
            total += dot(hot, tokens[...].astype(f32) * weight, 1, 0, lax.Precision.HIGHEST)
        router_part[...] = total
        each_z(lambda z: router_copy(z, me_z).start())
        router_z[me_z] = total

    def take_dx(h):
        dxs[h][1]()
        total = sum(
            dot(unperm[m], rd[h, m * dp : (m + 1) * dp].reshape(dp * cap, half), 1, 0)
            for m in range(members)
        )
        base = 2 * out_chunks + h * dx_chunks
        own[base : base + dx_chunks] = total.astype(bf).reshape(dx_chunks, chunk, half)

    def add_router():
        each_z(lambda z: router_copy(z, z).wait_recv())
        router_sum[...] = jnp.sum(router_z[...], axis=0)
        each_peer(lambda p: router_plane(p, me).start())
        router_mine.start()

    def line(source, target, send_sem, recv_sem, k, z_to):
        return remote(source.at[k], target.at[k], send_sem.at[k], recv_sem.at[k], {"expert": z_to})

    def step(t):
        ka = t - pos
        kb = t - (2 * mid + lag - pos)

        @pl.when((kb >= 0) & (kb < chunks))
        def _():
            @pl.when(pos == mid)
            def _():
                line(own, xch, xch_ss, xch_rs, kb, inner).wait()
                res[kb] = (own[kb].astype(f32) + xch[kb].astype(f32)).astype(bf)

            if mid > 1:

                @pl.when((pos < mid) & (pos > 0))
                def _():
                    line(res, res, res_ss, res_rs, kb, inner).wait_recv()

            @pl.when(pos > 0)
            def _():
                line(res, res, res_ss, res_rs, kb, outer).start()

        @pl.when(ka == 0)
        def _():
            take_out(0)

        @pl.when(ka == out_chunks)
        def _():
            loop(width // td, second_grads)
            store2.start()
            take_out(1)
            send_router()

        @pl.when(ka == 2 * out_chunks)
        def _():
            loop(width // td, first_grads)
            store1.start()
            add_router()
            take_dx(0)

        @pl.when(ka == 2 * out_chunks + dx_chunks)
        def _():
            take_dx(1)

        @pl.when((ka >= 0) & (ka < chunks))
        def _():
            @pl.when(pos > 0)
            def _():
                line(own, red, red_ss, red_rs, ka, outer).wait_recv()
                own[ka] = (own[ka].astype(f32) + red[ka].astype(f32)).astype(bf)

            @pl.when(pos < mid)
            def _():
                line(own, red, red_ss, red_rs, ka, inner).start()

            @pl.when(pos == mid)
            def _():
                line(own, xch, xch_ss, xch_rs, ka, inner).start()

    loop(chunks + 2 * mid + lag, step)

    def last_arrivals(k):
        @pl.when((pos < mid) & (pos == 0))
        def _():
            line(res, res, res_ss, res_rs, k, inner).wait_recv()

    loop(2 * out_chunks, last_arrivals)
    weights = []
    for m in range(members):
        total = jnp.zeros((toks, 1), f32)
        for h in range(2):
            cols = slice(h * half, (h + 1) * half)
            base = h * out_chunks + m * per_member
            value = res[base : base + per_member].reshape(toks, half).astype(f32)
            moe_out[m, :, cols] = (gates[m] * value).astype(bf)
            grad = out_grad[m, :, cols].astype(f32)
            total += jnp.sum(grad * value, axis=-1, keepdims=True)
        weights.append(total * gates[m] * (1.0 - gates[m]))
    loop(chunks - 2 * out_chunks, lambda k: last_arrivals(k + 2 * out_chunks))
    for h in range(2):
        cols = slice(h * half, (h + 1) * half)
        base = 2 * out_chunks + h * dx_chunks
        value = res[base : base + dx_chunks].reshape(toks, half).astype(f32)
        for m in range(members):
            value += weights[m] * picked_router[m, :, cols]
        token_grad[:, cols] = value

    def drain(k):
        @pl.when(pos < mid)
        def _():
            line(own, red, red_ss, red_rs, k, inner).wait_send()

        @pl.when(pos > 0)
        def _():
            line(res, res, res_ss, res_rs, k, outer).wait_send()

    loop(chunks, drain)
    x_finish()
    g_finish()
    for h in range(2):
        outs[h][2]()
        dxs[h][2]()
    store1.wait()
    store2.wait()
    each_z(lambda z: router_copy(z, me_z).wait_send())
    each_peer(lambda p: router_plane(p, me).wait_send())
    each_peer(lambda p: router_plane(p, p).wait_recv())
    router_mine.wait()


def shards(tokens, route_ids, router, w_in, w_out, out_grad):
    members, toks = route_ids.shape[:2]
    experts, width = router.shape[2], tokens.shape[1]
    dp, zn = lax.axis_size("dp"), lax.axis_size("expert")
    peers = dp * members
    hidden = w_in.shape[3]
    capacity = max(2, 3 * toks // (2 * experts))
    cap = -(-capacity // 16) * 16
    rows = peers * cap
    chunk = toks // 2
    half = width // 2
    bf, f32 = jnp.bfloat16, jnp.float32

    expert_ids = route_ids[:, :, 0]
    slots = slot_rank(expert_ids, experts)
    member_range = jnp.arange(members, dtype=jnp.int32)[:, None]
    col_place = expert_ids * cap + slots
    row_place = (expert_ids * members + member_range) * cap + slots

    vmem, anywhere = pl.BlockSpec(memory_space=pltpu.VMEM), pl.BlockSpec(memory_space=pl.ANY)
    chunks = 2 * (members + 1) * toks // chunk
    dma = pltpu.SemaphoreType.DMA
    block = pltpu.VMEM((peers, cap, width), bf)
    halves = pltpu.VMEM((2, peers, cap, half), bf)
    line = pltpu.VMEM((chunks, chunk, half), bf)
    router_shape = (members * experts, width)
    moe_out, token_grad, first, second, router_all = pl.pallas_call(
        functools.partial(layer_kernel, (dp, members, zn, cap, toks, chunk)),
        out_shape=(
            jax.ShapeDtypeStruct((members, toks, width), bf),
            jax.ShapeDtypeStruct((toks, width), f32),
            jax.ShapeDtypeStruct((width, hidden), bf),
            jax.ShapeDtypeStruct((hidden, width), bf),
            jax.ShapeDtypeStruct((peers,) + router_shape, f32),
        ),
        in_specs=[vmem] * 7 + [anywhere] * 2,
        out_specs=(vmem, vmem, anywhere, anywhere, anywhere),
        scratch_shapes=[
            block,
            block,
            pltpu.VMEM((members, rows, toks), bf),
            pltpu.VMEM((members, toks, dp * cap), bf),
            pltpu.VMEM((members, toks, width), f32),
            pltpu.VMEM((members, toks, 1), f32),
            pltpu.VMEM((members, toks, 1), f32),
            pltpu.VMEM((width, hidden), bf),
            pltpu.VMEM((hidden, width), bf),
            block,
            block,
            pltpu.VMEM((rows, hidden), bf),
            pltpu.VMEM((rows, hidden), f32),
            pltpu.VMEM((rows, hidden), bf),
            halves,
            halves,
            halves,
            halves,
            pltpu.VMEM((width, hidden), bf),
            pltpu.VMEM((hidden, width), bf),
            line,
            line,
            line,
            line,
            pltpu.VMEM(router_shape, f32),
            pltpu.VMEM((zn,) + router_shape, f32),
            pltpu.VMEM(router_shape, f32),
            dma((9,)),
        ]
        + [dma((peers,))] * 8
        + [dma((2, peers))] * 4
        + [dma((chunks,))] * 6
        + [dma((zn,))] * 2
        + [dma((peers,))] * 2,
        compiler_params=pltpu.CompilerParams(
            collective_id=0, has_side_effects=True, vmem_limit_bytes=60 * 1024 * 1024
        ),
        cost_estimate=pl.CostEstimate(
            flops=12 * rows * width * hidden,
            bytes_accessed=8 * width * hidden,
            transcendentals=rows * hidden,
        ),
    )(
        row_place[:, None, :],
        col_place[..., None],
        expert_ids[:, None, :],
        expert_ids[..., None],
        tokens,
        out_grad,
        jnp.swapaxes(router, 1, 2),
        w_in[0, 0],
        w_out[0, 0],
    )
    router_grad = jnp.swapaxes(
        jnp.sum(router_all, axis=0).reshape(members, experts, width), 1, 2
    )
    return (moe_out, token_grad, first[None, None], second[None, None], router_grad)


def solution(mesh):
    in_specs = (
        P(("dp", "member"), None),
        P(None, ("dp", "member"), None),
        P(),
        P("member", "dp", None, "expert"),
        P("member", "dp", "expert", None),
        P(None, ("dp", "member"), None),
    )
    out_specs = (
        P(None, ("dp", "member"), None),
        P(("dp", "member"), None),
        P("member", "dp", None, "expert"),
        P("member", "dp", "expert", None),
        P(),
    )
    return jax.shard_map(shards, mesh=mesh, in_specs=in_specs, out_specs=out_specs, check_vma=False)
```

```python
import functools

import jax
import jax.numpy as jnp
from jax import lax
from jax.experimental import pallas as pl
from jax.experimental.pallas import tpu as pltpu
from jax.sharding import PartitionSpec as P

MESH = pl.DeviceIdType.MESH
tanh_scale = 0.7978845608028654
cubic_term = 0.044715


def gelu_pair(pre_act):
    square = pre_act * pre_act
    tanh_value = jnp.tanh(tanh_scale * (pre_act + cubic_term * square * pre_act))
    half = 0.5 * (1.0 + tanh_value)
    slope = half + 0.5 * pre_act * (1.0 - tanh_value * tanh_value) * tanh_scale * (
        1.0 + 3.0 * cubic_term * square
    )
    return pre_act * half, slope


def dot(a, b, ca, cb, precision=None):
    return lax.dot_general(
        a, b, (((ca,), (cb,)), ((), ())), precision=precision, preferred_element_type=jnp.float32
    )


def tile_of(size, wanted):
    while size % wanted:
        wanted -= 128
    return wanted


def layer_kernel(
    cfg,
    row_ids, tokens, out_grad, router_t, w1_hbm, w2_hbm,
    moe_out, token_grad, first_hbm, second_hbm, router_all,
    x_send, g_send, picks, unperm, picked_router, gates, gate_grads,
    w1, w2, xr, gr, act, slope, pg, po, pd, ro, rd, first, second,
    own, red, xch, res, router_part, router_z, router_sum,
    load_sem, x_ss, x_rs, g_ss, g_rs, xf_ss, xf_rs, gf_ss, gf_rs, o_ss, o_rs, d_ss, d_rs,
    red_ss, red_rs, xch_ss, xch_rs, res_ss, res_rs, rz_ss, rz_rs, rp_ss, rp_rs,
):
    dp, members, zn, cap, toks, chunk = cfg
    peers = dp * members
    me_dp, me_m, me_z = lax.axis_index("dp"), lax.axis_index("member"), lax.axis_index("expert")
    me = me_dp * members + me_m
    width = x_send.shape[-1]
    half = width // 2
    hidden = w1.shape[1]
    rows = peers * cap
    experts = router_t.shape[1]
    bf, f32 = jnp.bfloat16, jnp.float32

    def plane(index):
        return {"dp": index // members, "member": index % members}

    def loop(count, body):
        lax.fori_loop(0, count, lambda i, c: (body(i), c)[1], 0)

    def flipped(index, bits):
        places = range(peers.bit_length() - 1)
        return sum(((index // (1 << b) + bits // (1 << b)) % 2) * (1 << b) for b in places)

    def each_peer(body):
        if peers & (peers - 1):
            loop(peers - 1, lambda i: body((me + 1 + i) % peers))
        else:
            turn = (peers // 2 - 1) * me_m
            loop(peers - 1, lambda i: body(flipped(me, (i + 1 + turn) % peers + (i + 1 + turn) // peers)))

    def each_z(body):
        loop(zn - 1, lambda i: body((me_z + 1 + i) % zn))

    def remote(source, target, send_sem, recv_sem, where):
        return pltpu.make_async_remote_copy(
            src_ref=source,
            dst_ref=target,
            send_sem=send_sem,
            recv_sem=recv_sem,
            device_id=where,
            device_id_type=MESH,
        )

    barrier = pltpu.get_barrier_semaphore()
    each_peer(
        lambda p: pl.semaphore_signal(barrier, inc=1, device_id=plane(p), device_id_type=MESH)
    )
    each_z(
        lambda z: pl.semaphore_signal(barrier, inc=1, device_id={"expert": z}, device_id_type=MESH)
    )
    load1 = pltpu.make_async_copy(w1_hbm, w1, load_sem.at[0])
    load2 = pltpu.make_async_copy(w2_hbm, w2, load_sem.at[1])
    load1.start()
    load2.start()

    relay = cap % 48 == 0
    third = cap // 3
    parity = me_z % 2
    partner = me_z + 1 - 2 * parity
    if relay:
        sent = pl.ds(pl.multiple_of(parity * third, 16), 2 * third)
        handed = pl.ds(pl.multiple_of(parity * 2 * third, 16), third)
        taken = pl.ds(pl.multiple_of((1 - parity) * 2 * third, 16), third)
    else:
        sent = pl.ds(0, cap)

    def dispatch(source, target, send_sem, recv_sem, relay_ss, relay_rs, own_sem):
        def send(peer, slot):
            return remote(
                source.at[peer, sent], target.at[slot, sent], send_sem.at[peer], recv_sem.at[slot], plane(peer)
            )

        def hand(peer, part):
            return remote(
                target.at[peer, part],
                target.at[peer, part],
                relay_ss.at[peer],
                relay_rs.at[peer],
                {"expert": partner},
            )

        mine = pltpu.make_async_copy(source.at[me], target.at[me], own_sem)

        def start():
            each_peer(lambda p: send(p, me).start())
            mine.start()

        def receive(then=None):
            def one(p):
                send(p, p).wait_recv()
                if relay:
                    hand(p, handed).start()

            each_peer(one)
            if then is not None:
                then()
            if relay:
                each_peer(lambda p: hand(p, taken).wait_recv())
            mine.wait()

        def finish():
            each_peer(lambda p: send(p, me).wait_send())
            if relay:
                each_peer(lambda p: hand(p, handed).wait_send())

        return start, receive, finish

    x_start, x_receive, x_finish = dispatch(x_send, xr, x_ss, x_rs, xf_ss, xf_rs, load_sem.at[2])
    g_start, g_receive, g_finish = dispatch(g_send, gr, g_ss, g_rs, gf_ss, gf_rs, load_sem.at[3])

    th = tile_of(hidden, 384)
    td = tile_of(width, 256)

    def count_up(shape, axis):
        return lax.broadcasted_iota(jnp.int32, shape, axis).astype(f32)

    down, across = count_up((toks, toks), 0), count_up((toks, toks), 1)
    row_index = count_up((rows, toks), 0)
    col_ids, col_slot = [], []
    for m in range(members):
        row_id = row_ids[m].astype(f32)
        col_id = jnp.sum(jnp.where(down == across, row_id, 0.0), axis=1, keepdims=True)
        same = (col_id == row_id).astype(f32)
        row_slot = jnp.sum(jnp.where(down < across, same, 0.0), axis=0, keepdims=True)
        col_slot.append(jnp.sum(jnp.where(across < down, same, 0.0), axis=1, keepdims=True))
        col_ids.append(col_id)
        row_place = (row_id * members + m) * cap + row_slot
        picks[m] = (row_index == row_place).astype(f32).astype(bf)

    def pack_tokens(j):
        cols = pl.ds(pl.multiple_of(j * td, 128), td)
        value = sum(dot(picks[m], tokens[:, cols], 1, 0) for m in range(members))
        x_send[:, :, cols] = value.astype(bf).reshape(peers, cap, td)

    loop(width // td, pack_tokens)
    pl.semaphore_wait(barrier, peers + zn - 2)
    x_start()

    hot_index = count_up((toks, experts), 1)
    tokens_f = tokens[...].astype(f32)
    for m in range(members):
        hot = (hot_index == col_ids[m]).astype(f32)
        picked_router[m] = dot(hot, router_t[m], 1, 0, lax.Precision.HIGHEST)
        logit = jnp.sum(tokens_f * picked_router[m], axis=-1, keepdims=True)
        gates[m] = 1.0 / (1.0 + jnp.exp(-logit))

    def pack_grads(j):
        cols = pl.ds(pl.multiple_of(j * td, 128), td)
        value = sum(
            dot(picks[m], (gates[m] * out_grad[m, :, cols].astype(f32)).astype(bf), 1, 0)
            for m in range(members)
        )
        g_send[:, :, cols] = value.astype(bf).reshape(peers, cap, td)

    loop(width // td, pack_grads)
    place_index = count_up((toks, dp * cap), 1)
    for m in range(members):
        unperm[m] = (place_index == col_ids[m] * cap + col_slot[m]).astype(f32).astype(bf)

    load1.wait()
    x_receive(g_start)

    def first_layer(j):
        cols = pl.ds(pl.multiple_of(j * th, 128), th)
        value, grad = gelu_pair(dot(xr[...].reshape(rows, width), w1[:, cols], 1, 0))
        act[:, cols] = value.astype(bf)
        slope[:, cols] = grad

    loop(hidden // th, first_layer)
    load2.wait()

    by_member = lambda d: (d % members) * dp + d // members

    def give_back(source, target, send_sem, recv_sem, h, own_sem):
        def send(peer, sender):
            return remote(
                source.at[h, peer],
                target.at[h, by_member(sender)],
                send_sem.at[h, peer],
                recv_sem.at[h, sender],
                plane(peer),
            )

        mine = pltpu.make_async_copy(source.at[h, me], target.at[h, by_member(me)], own_sem)

        def start():
            each_peer(lambda p: send(p, me).start())
            mine.start()

        def receive():
            each_peer(lambda p: send(p, p).wait_recv())
            mine.wait()

        return start, receive, lambda: each_peer(lambda p: send(p, me).wait_send())

    outs = [give_back(po, ro, o_ss, o_rs, h, load_sem.at[4 + h]) for h in range(2)]
    dxs = [give_back(pd, rd, d_ss, d_rs, h, load_sem.at[6 + h]) for h in range(2)]

    for h in range(2):
        part = dot(act[...], w2[:, h * half : (h + 1) * half], 1, 0).astype(bf)
        po[h] = part.reshape(peers, cap, half)
        if h == 0:
            outs[h][0]()

    g_receive(outs[1][0])

    def hidden_grad(j):
        cols = pl.ds(pl.multiple_of(j * th, 128), th)
        value = dot(gr[...].reshape(rows, width), w2[cols, :], 1, 1) * slope[:, cols]
        pg[:, cols] = value.astype(bf)

    loop(hidden // th, hidden_grad)
    for h in range(2):
        part = dot(pg[...], w1[h * half : (h + 1) * half, :], 1, 1).astype(bf)
        pd[h] = part.reshape(peers, cap, half)
        dxs[h][0]()

    mid = zn // 2 - 1
    left = me_z < zn // 2
    pos = jnp.where(left, me_z, zn - 1 - me_z)
    inner = jnp.where(left, me_z + 1, me_z - 1)
    outer = jnp.where(left, me_z - 1, me_z + 1)
    out_chunks = members * toks // chunk
    dx_chunks = toks // chunk
    chunks = 2 * (out_chunks + dx_chunks)
    per_member = toks // chunk
    lag = 2
    store1 = pltpu.make_async_copy(first, first_hbm, load_sem.at[0])
    store2 = pltpu.make_async_copy(second, second_hbm, load_sem.at[1])

    def router_copy(z_to, z_from):
        return remote(
            router_part, router_z.at[z_from], rz_ss.at[z_to], rz_rs.at[z_from], {"expert": z_to}
        )

    def router_plane(to, slot):
        return remote(router_sum, router_all.at[slot], rp_ss.at[to], rp_rs.at[slot], plane(to))

    router_mine = pltpu.make_async_copy(router_sum, router_all.at[me], load_sem.at[8])

    def second_grads(j):
        cols = pl.ds(pl.multiple_of(j * th, 128), th)
        second[cols, :] = dot(act[:, cols], gr[...].reshape(rows, width), 0, 0).astype(bf)

    def first_grads(j):
        cols = pl.ds(pl.multiple_of(j * td, 128), td)
        first[cols, :] = dot(xr[:, :, cols].reshape(rows, td), pg[...], 0, 0).astype(bf)

    def take_out(h):
        outs[h][1]()
        for m in range(members):
            part = dot(unperm[m], ro[h, m * dp : (m + 1) * dp].reshape(dp * cap, half), 1, 0)
            base = h * out_chunks + m * per_member
            own[base : base + per_member] = part.astype(bf).reshape(per_member, chunk, half)
            grad = out_grad[m, :, h * half : (h + 1) * half].astype(f32)
            partial = jnp.sum(grad * part, axis=-1, keepdims=True)
            gate_grads[m] = partial if h == 0 else gate_grads[m] + partial

    def send_router():
        total = jnp.zeros(router_part.shape, f32)
        hot_row = lax.broadcasted_iota(jnp.int32, (members * experts, toks), 0)
        for m in range(members):
            hot = (hot_row == row_ids[m] + m * experts).astype(f32)
            weight = gate_grads[m] * gates[m] * (1.0 - gates[m])
            total += dot(hot, tokens[...].astype(f32) * weight, 1, 0, lax.Precision.HIGHEST)
        router_part[...] = total
        each_z(lambda z: router_copy(z, me_z).start())
        router_z[me_z] = total

    def take_dx(h):
        dxs[h][1]()
        total = sum(
            dot(unperm[m], rd[h, m * dp : (m + 1) * dp].reshape(dp * cap, half), 1, 0)
            for m in range(members)
        )
        base = 2 * out_chunks + h * dx_chunks
        own[base : base + dx_chunks] = total.astype(bf).reshape(dx_chunks, chunk, half)

    def add_router():
        each_z(lambda z: router_copy(z, z).wait_recv())
        router_sum[...] = jnp.sum(router_z[...], axis=0)
        each_peer(lambda p: router_plane(p, me).start())
        router_mine.start()

    def line(source, target, send_sem, recv_sem, k, z_to):
        return remote(source.at[k], target.at[k], send_sem.at[k], recv_sem.at[k], {"expert": z_to})

    def step(t):
        ka = t - pos
        kb = t - (2 * mid + lag - pos)

        @pl.when((kb >= 0) & (kb < chunks))
        def _():
            @pl.when(pos == mid)
            def _():
                line(own, xch, xch_ss, xch_rs, kb, inner).wait()
                res[kb] = (own[kb].astype(f32) + xch[kb].astype(f32)).astype(bf)

            if mid > 1:

                @pl.when((pos < mid) & (pos > 0))
                def _():
                    line(res, res, res_ss, res_rs, kb, inner).wait_recv()

            @pl.when(pos > 0)
            def _():
                line(res, res, res_ss, res_rs, kb, outer).start()

        @pl.when(ka == 0)
        def _():
            take_out(0)

        @pl.when(ka == out_chunks)
        def _():
            loop(hidden // th, second_grads)
            store2.start()
            take_out(1)
            send_router()

        @pl.when(ka == 2 * out_chunks)
        def _():
            loop(width // td, first_grads)
            store1.start()
            add_router()
            take_dx(0)

        @pl.when(ka == 2 * out_chunks + dx_chunks)
        def _():
            take_dx(1)

        @pl.when((ka >= 0) & (ka < chunks))
        def _():
            @pl.when(pos > 0)
            def _():
                line(own, red, red_ss, red_rs, ka, outer).wait_recv()
                own[ka] = (own[ka].astype(f32) + red[ka].astype(f32)).astype(bf)

            @pl.when(pos < mid)
            def _():
                line(own, red, red_ss, red_rs, ka, inner).start()

            @pl.when(pos == mid)
            def _():
                line(own, xch, xch_ss, xch_rs, ka, inner).start()

    loop(chunks + 2 * mid + lag, step)

    def last_arrivals(k):
        @pl.when((pos < mid) & (pos == 0))
        def _():
            line(res, res, res_ss, res_rs, k, inner).wait_recv()

    loop(2 * out_chunks, last_arrivals)
    weights = []
    for m in range(members):
        total = jnp.zeros((toks, 1), f32)
        for h in range(2):
            cols = slice(h * half, (h + 1) * half)
            base = h * out_chunks + m * per_member
            value = res[base : base + per_member].reshape(toks, half).astype(f32)
            moe_out[m, :, cols] = (gates[m] * value).astype(bf)
            grad = out_grad[m, :, cols].astype(f32)
            total += jnp.sum(grad * value, axis=-1, keepdims=True)
        weights.append(total * gates[m] * (1.0 - gates[m]))
    loop(chunks - 2 * out_chunks, lambda k: last_arrivals(k + 2 * out_chunks))
    for h in range(2):
        cols = slice(h * half, (h + 1) * half)
        base = 2 * out_chunks + h * dx_chunks
        value = res[base : base + dx_chunks].reshape(toks, half).astype(f32)
        for m in range(members):
            value += weights[m] * picked_router[m, :, cols]
        token_grad[:, cols] = value

    def drain(k):
        @pl.when(pos < mid)
        def _():
            line(own, red, red_ss, red_rs, k, inner).wait_send()

        @pl.when(pos > 0)
        def _():
            line(res, res, res_ss, res_rs, k, outer).wait_send()

    loop(chunks, drain)
    x_finish()
    g_finish()
    for h in range(2):
        outs[h][2]()
        dxs[h][2]()
    store1.wait()
    store2.wait()
    each_z(lambda z: router_copy(z, me_z).wait_send())
    each_peer(lambda p: router_plane(p, me).wait_send())
    each_peer(lambda p: router_plane(p, p).wait_recv())
    router_mine.wait()


parts = 4


def write_out(moe, grad, first, second, routers, moe_to, grad_to, first_to, second_to, router_to, sem):
    copies = []
    for source, target in ((first, first_to), (second, second_to)):
        size = source.shape[0] // parts
        for k in range(parts):
            piece = pl.ds(k * size, size)
            copies.append((source.at[piece], target.at[piece]))
    copies += [(moe, moe_to), (grad, grad_to)]
    copies = [pltpu.make_async_copy(a, b, sem.at[k]) for k, (a, b) in enumerate(copies)]
    for copy in copies:
        copy.start()
    total = jnp.sum(routers[...], axis=0)
    members, experts = router_to.shape[:2]
    for m in range(members):
        router_to[m] = total[m * experts : (m + 1) * experts]
    for copy in copies:
        copy.wait()


def shards(tokens, route_ids, router, w_in, w_out, out_grad):
    members, toks = route_ids.shape[:2]
    experts, width = router.shape[2], tokens.shape[1]
    dp, zn = lax.axis_size("dp"), lax.axis_size("expert")
    peers = dp * members
    hidden = w_in.shape[3]
    capacity = max(2, 3 * toks // (2 * experts))
    cap = -(-capacity // 16) * 16
    rows = peers * cap
    chunk = toks // 4
    half = width // 2
    bf, f32 = jnp.bfloat16, jnp.float32

    vmem, anywhere = pl.BlockSpec(memory_space=pltpu.VMEM), pl.BlockSpec(memory_space=pl.ANY)
    chunks = 2 * (members + 1) * toks // chunk
    dma = pltpu.SemaphoreType.DMA
    block = pltpu.VMEM((peers, cap, width), bf)
    halves = pltpu.VMEM((2, peers, cap, half), bf)
    line = pltpu.VMEM((chunks, chunk, half), bf)
    router_shape = (members * experts, width)
    moe_out, token_grad, first, second, router_all = pl.pallas_call(
        functools.partial(layer_kernel, (dp, members, zn, cap, toks, chunk)),
        out_shape=(
            jax.ShapeDtypeStruct((members, toks, width), bf),
            jax.ShapeDtypeStruct((toks, width), f32),
            jax.ShapeDtypeStruct((width, hidden), bf),
            jax.ShapeDtypeStruct((hidden, width), bf),
            jax.ShapeDtypeStruct((peers,) + router_shape, f32),
        ),
        in_specs=[vmem] * 4 + [anywhere] * 2,
        out_specs=(vmem, vmem, anywhere, anywhere, anywhere),
        scratch_shapes=[
            block,
            block,
            pltpu.VMEM((members, rows, toks), bf),
            pltpu.VMEM((members, toks, dp * cap), bf),
            pltpu.VMEM((members, toks, width), f32),
            pltpu.VMEM((members, toks, 1), f32),
            pltpu.VMEM((members, toks, 1), f32),
            pltpu.VMEM((width, hidden), bf),
            pltpu.VMEM((hidden, width), bf),
            block,
            block,
            pltpu.VMEM((rows, hidden), bf),
            pltpu.VMEM((rows, hidden), f32),
            pltpu.VMEM((rows, hidden), bf),
            halves,
            halves,
            halves,
            halves,
            pltpu.VMEM((width, hidden), bf),
            pltpu.VMEM((hidden, width), bf),
            line,
            line,
            line,
            line,
            pltpu.VMEM(router_shape, f32),
            pltpu.VMEM((zn,) + router_shape, f32),
            pltpu.VMEM(router_shape, f32),
            dma((9,)),
        ]
        + [dma((peers,))] * 8
        + [dma((2, peers))] * 4
        + [dma((chunks,))] * 6
        + [dma((zn,))] * 2
        + [dma((peers,))] * 2,
        compiler_params=pltpu.CompilerParams(
            collective_id=0, has_side_effects=True, vmem_limit_bytes=60 * 1024 * 1024
        ),
        cost_estimate=pl.CostEstimate(
            flops=12 * rows * width * hidden,
            bytes_accessed=8 * width * hidden,
            transcendentals=rows * hidden,
        ),
    )(
        jnp.swapaxes(route_ids, 1, 2),
        tokens,
        out_grad,
        jnp.swapaxes(router, 1, 2),
        w_in[0, 0],
        w_out[0, 0],
    )
    finals = (moe_out, token_grad, first, second)
    moe_out, token_grad, first, second, router_sum = pl.pallas_call(
        write_out,
        out_shape=tuple(jax.ShapeDtypeStruct(v.shape, v.dtype) for v in finals)
        + (jax.ShapeDtypeStruct((members, experts, width), f32),),
        in_specs=[anywhere] * 4 + [vmem],
        out_specs=(anywhere,) * 4 + (vmem,),
        scratch_shapes=[dma((2 + 2 * parts,))],
        compiler_params=pltpu.CompilerParams(vmem_limit_bytes=60 * 1024 * 1024),
    )(*finals, router_all)
    router_grad = jnp.swapaxes(router_sum, 1, 2)
    return (moe_out, token_grad, first[None, None], second[None, None], router_grad)


def solution(mesh):
    in_specs = (
        P(("dp", "member"), None),
        P(None, ("dp", "member"), None),
        P(),
        P("member", "dp", None, "expert"),
        P("member", "dp", "expert", None),
        P(None, ("dp", "member"), None),
    )
    out_specs = (
        P(None, ("dp", "member"), None),
        P(("dp", "member"), None),
        P("member", "dp", None, "expert"),
        P("member", "dp", "expert", None),
        P(),
    )
    return jax.shard_map(shards, mesh=mesh, in_specs=in_specs, out_specs=out_specs, check_vma=False)
```

```python
import functools

import jax
import jax.numpy as jnp
from jax import lax
from jax.experimental import pallas as pl
from jax.experimental.pallas import tpu as pltpu
from jax.sharding import PartitionSpec as P

MESH = pl.DeviceIdType.MESH
tanh_scale = 0.7978845608028654
cubic_term = 0.044715


def gelu_pair(pre_act):
    square = pre_act * pre_act
    tanh_value = jnp.tanh(tanh_scale * (pre_act + cubic_term * square * pre_act))
    half = 0.5 * (1.0 + tanh_value)
    slope = half + 0.5 * pre_act * (1.0 - tanh_value * tanh_value) * tanh_scale * (
        1.0 + 3.0 * cubic_term * square
    )
    return pre_act * half, slope


def dot(a, b, ca, cb, precision=None):
    return lax.dot_general(
        a, b, (((ca,), (cb,)), ((), ())), precision=precision, preferred_element_type=jnp.float32
    )


def tile_of(size, wanted):
    while size % wanted:
        wanted -= 128
    return wanted


def layer_kernel(
    cfg,
    row_ids, tokens, out_grad, router_t, w1_hbm, w2_hbm,
    moe_out, token_grad, first_hbm, second_hbm, router_all,
    x_send, g_send, picks, unperm, picked_router, gates, gate_grads,
    w1, w2, xr, gr, act, slope, pg, po, pd, ro, rd, first, second,
    own, red, xch, res, router_part, router_z, router_sum,
    load_sem, x_ss, x_rs, g_ss, g_rs, xf_ss, xf_rs, gf_ss, gf_rs, o_ss, o_rs, d_ss, d_rs,
    red_ss, red_rs, xch_ss, xch_rs, res_ss, res_rs, rz_ss, rz_rs, rp_ss, rp_rs,
):
    dp, members, zn, cap, toks, chunk = cfg
    peers = dp * members
    me_dp, me_m, me_z = lax.axis_index("dp"), lax.axis_index("member"), lax.axis_index("expert")
    me = me_dp * members + me_m
    width = x_send.shape[-1]
    half = width // 2
    hidden = w1.shape[1]
    rows = peers * cap
    experts = router_t.shape[1]
    bf, f32 = jnp.bfloat16, jnp.float32

    def plane(index):
        return {"dp": index // members, "member": index % members}

    def loop(count, body):
        lax.fori_loop(0, count, lambda i, c: (body(i), c)[1], 0)

    def each_peer(body):
        loop(peers - 1, lambda i: body((me + 1 + i) % peers))

    def each_z(body):
        loop(zn - 1, lambda i: body((me_z + 1 + i) % zn))

    def remote(source, target, send_sem, recv_sem, where):
        return pltpu.make_async_remote_copy(
            src_ref=source,
            dst_ref=target,
            send_sem=send_sem,
            recv_sem=recv_sem,
            device_id=where,
            device_id_type=MESH,
        )

    barrier = pltpu.get_barrier_semaphore()
    each_peer(
        lambda p: pl.semaphore_signal(barrier, inc=1, device_id=plane(p), device_id_type=MESH)
    )
    each_z(
        lambda z: pl.semaphore_signal(barrier, inc=1, device_id={"expert": z}, device_id_type=MESH)
    )
    load1 = pltpu.make_async_copy(w1_hbm, w1, load_sem.at[0])
    load2 = pltpu.make_async_copy(w2_hbm, w2, load_sem.at[1])
    load1.start()
    load2.start()

    relay = cap % 48 == 0
    third = cap // 3
    parity = me_z % 2
    partner = me_z + 1 - 2 * parity
    if relay:
        sent = pl.ds(pl.multiple_of(parity * third, 16), 2 * third)
        handed = pl.ds(pl.multiple_of(parity * 2 * third, 16), third)
        taken = pl.ds(pl.multiple_of((1 - parity) * 2 * third, 16), third)
    else:
        sent = pl.ds(0, cap)

    def dispatch(source, target, send_sem, recv_sem, relay_ss, relay_rs, own_sem):
        def send(peer, slot):
            return remote(
                source.at[peer, sent], target.at[slot, sent], send_sem.at[peer], recv_sem.at[slot], plane(peer)
            )

        def hand(peer, part):
            return remote(
                target.at[peer, part],
                target.at[peer, part],
                relay_ss.at[peer],
                relay_rs.at[peer],
                {"expert": partner},
            )

        mine = pltpu.make_async_copy(source.at[me], target.at[me], own_sem)

        def start():
            each_peer(lambda p: send(p, me).start())
            mine.start()

        def receive():
            def one(p):
                send(p, p).wait_recv()
                if relay:
                    hand(p, handed).start()

            each_peer(one)
            if relay:
                each_peer(lambda p: hand(p, taken).wait_recv())
            mine.wait()

        def finish():
            each_peer(lambda p: send(p, me).wait_send())
            if relay:
                each_peer(lambda p: hand(p, handed).wait_send())

        return start, receive, finish

    x_start, x_receive, x_finish = dispatch(x_send, xr, x_ss, x_rs, xf_ss, xf_rs, load_sem.at[2])
    g_start, g_receive, g_finish = dispatch(g_send, gr, g_ss, g_rs, gf_ss, gf_rs, load_sem.at[3])

    th = tile_of(hidden, 384)
    td = tile_of(width, 256)

    def count_up(shape, axis):
        return lax.broadcasted_iota(jnp.int32, shape, axis).astype(f32)

    down, across = count_up((toks, toks), 0), count_up((toks, toks), 1)
    row_index = count_up((rows, toks), 0)
    col_ids, col_slot = [], []
    for m in range(members):
        row_id = row_ids[m].astype(f32)
        col_id = jnp.sum(jnp.where(down == across, row_id, 0.0), axis=1, keepdims=True)
        same = (col_id == row_id).astype(f32)
        row_slot = jnp.sum(jnp.where(down < across, same, 0.0), axis=0, keepdims=True)
        col_slot.append(jnp.sum(jnp.where(across < down, same, 0.0), axis=1, keepdims=True))
        col_ids.append(col_id)
        row_place = (row_id * members + m) * cap + row_slot
        picks[m] = (row_index == row_place).astype(f32).astype(bf)

    def pack_tokens(j):
        cols = pl.ds(pl.multiple_of(j * td, 128), td)
        value = sum(dot(picks[m], tokens[:, cols], 1, 0) for m in range(members))
        x_send[:, :, cols] = value.astype(bf).reshape(peers, cap, td)

    loop(width // td, pack_tokens)
    pl.semaphore_wait(barrier, peers + zn - 2)
    x_start()

    hot_index = count_up((toks, experts), 1)
    tokens_f = tokens[...].astype(f32)
    for m in range(members):
        hot = (hot_index == col_ids[m]).astype(f32)
        picked_router[m] = dot(hot, router_t[m], 1, 0, lax.Precision.HIGHEST)
        logit = jnp.sum(tokens_f * picked_router[m], axis=-1, keepdims=True)
        gates[m] = 1.0 / (1.0 + jnp.exp(-logit))

    def pack_grads(j):
        cols = pl.ds(pl.multiple_of(j * td, 128), td)
        value = sum(
            dot(picks[m], (gates[m] * out_grad[m, :, cols].astype(f32)).astype(bf), 1, 0)
            for m in range(members)
        )
        g_send[:, :, cols] = value.astype(bf).reshape(peers, cap, td)

    loop(width // td, pack_grads)
    g_start()
    place_index = count_up((toks, dp * cap), 1)
    for m in range(members):
        unperm[m] = (place_index == col_ids[m] * cap + col_slot[m]).astype(f32).astype(bf)

    load1.wait()
    x_receive()

    def first_layer(j):
        cols = pl.ds(pl.multiple_of(j * th, 128), th)
        value, grad = gelu_pair(dot(xr[...].reshape(rows, width), w1[:, cols], 1, 0))
        act[:, cols] = value.astype(bf)
        slope[:, cols] = grad

    loop(hidden // th, first_layer)
    load2.wait()

    by_member = lambda d: (d % members) * dp + d // members

    def give_back(source, target, send_sem, recv_sem, h, own_sem):
        def send(peer, sender):
            return remote(
                source.at[h, peer],
                target.at[h, by_member(sender)],
                send_sem.at[h, peer],
                recv_sem.at[h, sender],
                plane(peer),
            )

        mine = pltpu.make_async_copy(source.at[h, me], target.at[h, by_member(me)], own_sem)

        def start():
            each_peer(lambda p: send(p, me).start())
            mine.start()

        def receive():
            each_peer(lambda p: send(p, p).wait_recv())
            mine.wait()

        return start, receive, lambda: each_peer(lambda p: send(p, me).wait_send())

    outs = [give_back(po, ro, o_ss, o_rs, h, load_sem.at[4 + h]) for h in range(2)]
    dxs = [give_back(pd, rd, d_ss, d_rs, h, load_sem.at[6 + h]) for h in range(2)]

    for h in range(2):
        part = dot(act[...], w2[:, h * half : (h + 1) * half], 1, 0).astype(bf)
        po[h] = part.reshape(peers, cap, half)
        outs[h][0]()

    g_receive()

    def hidden_grad(j):
        cols = pl.ds(pl.multiple_of(j * th, 128), th)
        value = dot(gr[...].reshape(rows, width), w2[cols, :], 1, 1) * slope[:, cols]
        pg[:, cols] = value.astype(bf)

    loop(hidden // th, hidden_grad)
    for h in range(2):
        part = dot(pg[...], w1[h * half : (h + 1) * half, :], 1, 1).astype(bf)
        pd[h] = part.reshape(peers, cap, half)
        dxs[h][0]()

    mid = zn // 2 - 1
    left = me_z < zn // 2
    pos = jnp.where(left, me_z, zn - 1 - me_z)
    inner = jnp.where(left, me_z + 1, me_z - 1)
    outer = jnp.where(left, me_z - 1, me_z + 1)
    out_chunks = members * toks // chunk
    dx_chunks = toks // chunk
    chunks = 2 * (out_chunks + dx_chunks)
    per_member = toks // chunk
    lag = 2
    store1 = pltpu.make_async_copy(first, first_hbm, load_sem.at[0])
    store2 = pltpu.make_async_copy(second, second_hbm, load_sem.at[1])

    def router_copy(z_to, z_from):
        return remote(
            router_part, router_z.at[z_from], rz_ss.at[z_to], rz_rs.at[z_from], {"expert": z_to}
        )

    def router_plane(to, slot):
        return remote(router_sum, router_all.at[slot], rp_ss.at[to], rp_rs.at[slot], plane(to))

    router_mine = pltpu.make_async_copy(router_sum, router_all.at[me], load_sem.at[8])

    def second_grads(j):
        cols = pl.ds(pl.multiple_of(j * th, 128), th)
        second[cols, :] = dot(act[:, cols], gr[...].reshape(rows, width), 0, 0).astype(bf)

    def first_grads(j):
        cols = pl.ds(pl.multiple_of(j * td, 128), td)
        first[cols, :] = dot(xr[:, :, cols].reshape(rows, td), pg[...], 0, 0).astype(bf)

    def take_out(h):
        outs[h][1]()
        for m in range(members):
            part = dot(unperm[m], ro[h, m * dp : (m + 1) * dp].reshape(dp * cap, half), 1, 0)
            base = h * out_chunks + m * per_member
            own[base : base + per_member] = part.astype(bf).reshape(per_member, chunk, half)
            grad = out_grad[m, :, h * half : (h + 1) * half].astype(f32)
            partial = jnp.sum(grad * part, axis=-1, keepdims=True)
            gate_grads[m] = partial if h == 0 else gate_grads[m] + partial

    def send_router():
        total = jnp.zeros(router_part.shape, f32)
        hot_row = lax.broadcasted_iota(jnp.int32, (members * experts, toks), 0)
        for m in range(members):
            hot = (hot_row == row_ids[m] + m * experts).astype(f32)
            weight = gate_grads[m] * gates[m] * (1.0 - gates[m])
            total += dot(hot, tokens[...].astype(f32) * weight, 1, 0, lax.Precision.HIGHEST)
        router_part[...] = total
        each_z(lambda z: router_copy(z, me_z).start())
        router_z[me_z] = total

    def take_dx(h):
        dxs[h][1]()
        total = sum(
            dot(unperm[m], rd[h, m * dp : (m + 1) * dp].reshape(dp * cap, half), 1, 0)
            for m in range(members)
        )
        base = 2 * out_chunks + h * dx_chunks
        own[base : base + dx_chunks] = total.astype(bf).reshape(dx_chunks, chunk, half)

    def add_router():
        each_z(lambda z: router_copy(z, z).wait_recv())
        router_sum[...] = jnp.sum(router_z[...], axis=0)
        each_peer(lambda p: router_plane(p, me).start())
        router_mine.start()

    def line(source, target, send_sem, recv_sem, k, z_to):
        return remote(source.at[k], target.at[k], send_sem.at[k], recv_sem.at[k], {"expert": z_to})

    def step(t):
        ka = t - pos
        kb = t - (2 * mid + lag - pos)

        @pl.when((kb >= 0) & (kb < chunks))
        def _():
            @pl.when(pos == mid)
            def _():
                line(own, xch, xch_ss, xch_rs, kb, inner).wait()
                res[kb] = (own[kb].astype(f32) + xch[kb].astype(f32)).astype(bf)

            if mid > 1:

                @pl.when((pos < mid) & (pos > 0))
                def _():
                    line(res, res, res_ss, res_rs, kb, inner).wait_recv()

            @pl.when(pos > 0)
            def _():
                line(res, res, res_ss, res_rs, kb, outer).start()

        @pl.when(ka == 0)
        def _():
            take_out(0)

        @pl.when(ka == out_chunks)
        def _():
            loop(hidden // th, second_grads)
            store2.start()
            take_out(1)
            send_router()

        @pl.when(ka == 2 * out_chunks)
        def _():
            loop(width // td, first_grads)
            store1.start()
            add_router()
            take_dx(0)

        @pl.when(ka == 2 * out_chunks + dx_chunks)
        def _():
            take_dx(1)

        @pl.when((ka >= 0) & (ka < chunks))
        def _():
            @pl.when(pos > 0)
            def _():
                line(own, red, red_ss, red_rs, ka, outer).wait_recv()
                own[ka] = (own[ka].astype(f32) + red[ka].astype(f32)).astype(bf)

            @pl.when(pos < mid)
            def _():
                line(own, red, red_ss, red_rs, ka, inner).start()

            @pl.when(pos == mid)
            def _():
                line(own, xch, xch_ss, xch_rs, ka, inner).start()

    loop(chunks + 2 * mid + lag, step)

    def last_arrivals(k):
        @pl.when((pos < mid) & (pos == 0))
        def _():
            line(res, res, res_ss, res_rs, k, inner).wait_recv()

    loop(2 * out_chunks, last_arrivals)
    weights = []
    for m in range(members):
        total = jnp.zeros((toks, 1), f32)
        for h in range(2):
            cols = slice(h * half, (h + 1) * half)
            base = h * out_chunks + m * per_member
            value = res[base : base + per_member].reshape(toks, half).astype(f32)
            moe_out[m, :, cols] = (gates[m] * value).astype(bf)
            grad = out_grad[m, :, cols].astype(f32)
            total += jnp.sum(grad * value, axis=-1, keepdims=True)
        weights.append(total * gates[m] * (1.0 - gates[m]))
    loop(chunks - 2 * out_chunks, lambda k: last_arrivals(k + 2 * out_chunks))
    for h in range(2):
        cols = slice(h * half, (h + 1) * half)
        base = 2 * out_chunks + h * dx_chunks
        value = res[base : base + dx_chunks].reshape(toks, half).astype(f32)
        for m in range(members):
            value += weights[m] * picked_router[m, :, cols]
        token_grad[:, cols] = value

    def drain(k):
        @pl.when(pos < mid)
        def _():
            line(own, red, red_ss, red_rs, k, inner).wait_send()

        @pl.when(pos > 0)
        def _():
            line(res, res, res_ss, res_rs, k, outer).wait_send()

    loop(chunks, drain)
    x_finish()
    g_finish()
    for h in range(2):
        outs[h][2]()
        dxs[h][2]()
    store1.wait()
    store2.wait()
    each_z(lambda z: router_copy(z, me_z).wait_send())
    each_peer(lambda p: router_plane(p, me).wait_send())
    each_peer(lambda p: router_plane(p, p).wait_recv())
    router_mine.wait()


parts = 4


def write_out(moe, grad, first, second, routers, moe_to, grad_to, first_to, second_to, router_to):
    moe_to[...] = moe[...]
    grad_to[...] = grad[...]
    first_to[...] = first[...]
    second_to[...] = second[...]

    @pl.when(pl.program_id(0) == 0)
    def _():
        total = jnp.sum(routers[...], axis=0)
        members, experts = router_to.shape[:2]
        for m in range(members):
            router_to[m] = total[m * experts : (m + 1) * experts]


def shards(tokens, route_ids, router, w_in, w_out, out_grad):
    members, toks = route_ids.shape[:2]
    experts, width = router.shape[2], tokens.shape[1]
    dp, zn = lax.axis_size("dp"), lax.axis_size("expert")
    peers = dp * members
    hidden = w_in.shape[3]
    capacity = max(2, 3 * toks // (2 * experts))
    cap = -(-capacity // 16) * 16
    rows = peers * cap
    chunk = toks // 2
    half = width // 2
    bf, f32 = jnp.bfloat16, jnp.float32

    vmem, anywhere = pl.BlockSpec(memory_space=pltpu.VMEM), pl.BlockSpec(memory_space=pl.ANY)
    chunks = 2 * (members + 1) * toks // chunk
    dma = pltpu.SemaphoreType.DMA
    block = pltpu.VMEM((peers, cap, width), bf)
    halves = pltpu.VMEM((2, peers, cap, half), bf)
    line = pltpu.VMEM((chunks, chunk, half), bf)
    router_shape = (members * experts, width)
    moe_out, token_grad, first, second, router_all = pl.pallas_call(
        functools.partial(layer_kernel, (dp, members, zn, cap, toks, chunk)),
        out_shape=(
            jax.ShapeDtypeStruct((members, toks, width), bf),
            jax.ShapeDtypeStruct((toks, width), f32),
            jax.ShapeDtypeStruct((width, hidden), bf),
            jax.ShapeDtypeStruct((hidden, width), bf),
            jax.ShapeDtypeStruct((peers,) + router_shape, f32),
        ),
        in_specs=[vmem] * 4 + [anywhere] * 2,
        out_specs=(vmem, vmem, anywhere, anywhere, anywhere),
        scratch_shapes=[
            block,
            block,
            pltpu.VMEM((members, rows, toks), bf),
            pltpu.VMEM((members, toks, dp * cap), bf),
            pltpu.VMEM((members, toks, width), f32),
            pltpu.VMEM((members, toks, 1), f32),
            pltpu.VMEM((members, toks, 1), f32),
            pltpu.VMEM((width, hidden), bf),
            pltpu.VMEM((hidden, width), bf),
            block,
            block,
            pltpu.VMEM((rows, hidden), bf),
            pltpu.VMEM((rows, hidden), f32),
            pltpu.VMEM((rows, hidden), bf),
            halves,
            halves,
            halves,
            halves,
            pltpu.VMEM((width, hidden), bf),
            pltpu.VMEM((hidden, width), bf),
            line,
            line,
            line,
            line,
            pltpu.VMEM(router_shape, f32),
            pltpu.VMEM((zn,) + router_shape, f32),
            pltpu.VMEM(router_shape, f32),
            dma((9,)),
        ]
        + [dma((peers,))] * 8
        + [dma((2, peers))] * 4
        + [dma((chunks,))] * 6
        + [dma((zn,))] * 2
        + [dma((peers,))] * 2,
        compiler_params=pltpu.CompilerParams(
            collective_id=0, has_side_effects=True, vmem_limit_bytes=60 * 1024 * 1024
        ),
        cost_estimate=pl.CostEstimate(
            flops=12 * rows * width * hidden,
            bytes_accessed=8 * width * hidden,
            transcendentals=rows * hidden,
        ),
    )(
        jnp.swapaxes(route_ids, 1, 2),
        tokens,
        out_grad,
        jnp.swapaxes(router, 1, 2),
        w_in[0, 0],
        w_out[0, 0],
    )
    finals = (moe_out, token_grad, first, second)
    pieces = [
        pl.BlockSpec((members, toks // parts, width), lambda i: (0, i, 0)),
        pl.BlockSpec((toks // parts, width), lambda i: (i, 0)),
        pl.BlockSpec((width // parts, hidden), lambda i: (i, 0)),
        pl.BlockSpec((hidden // parts, width), lambda i: (i, 0)),
    ]
    moe_out, token_grad, first, second, router_sum = pl.pallas_call(
        write_out,
        grid=(parts,),
        out_shape=tuple(jax.ShapeDtypeStruct(v.shape, v.dtype) for v in finals)
        + (jax.ShapeDtypeStruct((members, experts, width), f32),),
        in_specs=pieces + [pl.BlockSpec(router_all.shape, lambda i: (0, 0, 0))],
        out_specs=tuple(pieces) + (pl.BlockSpec((members, experts, width), lambda i: (0, 0, 0)),),
        compiler_params=pltpu.CompilerParams(vmem_limit_bytes=60 * 1024 * 1024),
    )(*finals, router_all)
    router_grad = jnp.swapaxes(router_sum, 1, 2)
    return (moe_out, token_grad, first[None, None], second[None, None], router_grad)


def solution(mesh):
    in_specs = (
        P(("dp", "member"), None),
        P(None, ("dp", "member"), None),
        P(),
        P("member", "dp", None, "expert"),
        P("member", "dp", "expert", None),
        P(None, ("dp", "member"), None),
    )
    out_specs = (
        P(None, ("dp", "member"), None),
        P(("dp", "member"), None),
        P("member", "dp", None, "expert"),
        P("member", "dp", "expert", None),
        P(),
    )
    return jax.shard_map(shards, mesh=mesh, in_specs=in_specs, out_specs=out_specs, check_vma=False)
```

```python
import functools

import jax
import jax.numpy as jnp
from jax import lax
from jax.experimental import pallas as pl
from jax.experimental.pallas import tpu as pltpu
from jax.sharding import PartitionSpec as P

MESH = pl.DeviceIdType.MESH
tanh_scale = 0.7978845608028654
cubic_term = 0.044715


def gelu_pair(pre_act):
    square = pre_act * pre_act
    tanh_value = jnp.tanh(tanh_scale * (pre_act + cubic_term * square * pre_act))
    half = 0.5 * (1.0 + tanh_value)
    slope = half + 0.5 * pre_act * (1.0 - tanh_value * tanh_value) * tanh_scale * (
        1.0 + 3.0 * cubic_term * square
    )
    return pre_act * half, slope


def dot(a, b, ca, cb, precision=None):
    return lax.dot_general(
        a, b, (((ca,), (cb,)), ((), ())), precision=precision, preferred_element_type=jnp.float32
    )


def tile_of(size, wanted):
    while size % wanted:
        wanted -= 128
    return wanted


def layer_kernel(
    cfg,
    row_ids, tokens, out_grad, router_t, w1_hbm, w2_hbm,
    moe_out, token_grad, first_hbm, second_hbm, router_all,
    x_send, g_send, picks, unperm, picked_router, gates, gate_grads,
    w1, w2, xr, gr, act, slope, pg, po, pd, ro, rd, first, second,
    own, red, xch, res, router_part, router_in, router_row, router_z, router_sum,
    load_sem, x_ss, x_rs, g_ss, g_rs, xf_ss, xf_rs, gf_ss, gf_rs, o_ss, o_rs, d_ss, d_rs,
    red_ss, red_rs, xch_ss, xch_rs, res_ss, res_rs, rz_ss, rz_rs, rp_ss, rp_rs, ri_ss, ri_rs,
):
    dp, members, zn, cap, toks, chunk = cfg
    peers = dp * members
    me_dp, me_m, me_z = lax.axis_index("dp"), lax.axis_index("member"), lax.axis_index("expert")
    me = me_dp * members + me_m
    width = x_send.shape[-1]
    half = width // 2
    hidden = w1.shape[1]
    rows = peers * cap
    experts = router_t.shape[1]
    bf, f32 = jnp.bfloat16, jnp.float32

    def plane(index):
        return {"dp": index // members, "member": index % members}

    def loop(count, body):
        lax.fori_loop(0, count, lambda i, c: (body(i), c)[1], 0)

    def each_peer(body):
        loop(peers - 1, lambda i: body((me + 1 + (i + 1 - me_m) % (peers - 1)) % peers))

    def each_z(body):
        loop(zn - 1, lambda i: body((me_z + 1 + i) % zn))

    def remote(source, target, send_sem, recv_sem, where):
        return pltpu.make_async_remote_copy(
            src_ref=source,
            dst_ref=target,
            send_sem=send_sem,
            recv_sem=recv_sem,
            device_id=where,
            device_id_type=MESH,
        )

    barrier = pltpu.get_barrier_semaphore()
    each_peer(
        lambda p: pl.semaphore_signal(barrier, inc=1, device_id=plane(p), device_id_type=MESH)
    )
    each_z(
        lambda z: pl.semaphore_signal(barrier, inc=1, device_id={"expert": z}, device_id_type=MESH)
    )
    load1 = pltpu.make_async_copy(w1_hbm, w1, load_sem.at[0])
    load2 = pltpu.make_async_copy(w2_hbm, w2, load_sem.at[1])
    load1.start()
    load2.start()

    relay = cap % 48 == 0
    third = cap // 3
    parity = me_z % 2
    partner = me_z + 1 - 2 * parity
    if relay:
        sent = pl.ds(pl.multiple_of(parity * third, 16), 2 * third)
        handed = pl.ds(pl.multiple_of(parity * 2 * third, 16), third)
        taken = pl.ds(pl.multiple_of((1 - parity) * 2 * third, 16), third)
    else:
        sent = pl.ds(0, cap)

    def dispatch(source, target, send_sem, recv_sem, relay_ss, relay_rs, own_sem):
        def send(peer, slot):
            return remote(
                source.at[peer, sent], target.at[slot, sent], send_sem.at[peer], recv_sem.at[slot], plane(peer)
            )

        def hand(peer, part):
            return remote(
                target.at[peer, part],
                target.at[peer, part],
                relay_ss.at[peer],
                relay_rs.at[peer],
                {"expert": partner},
            )

        mine = pltpu.make_async_copy(source.at[me], target.at[me], own_sem)

        def start():
            each_peer(lambda p: send(p, me).start())
            mine.start()

        def receive():
            def one(p):
                send(p, p).wait_recv()
                if relay:
                    hand(p, handed).start()

            each_peer(one)
            if relay:
                each_peer(lambda p: hand(p, taken).wait_recv())
            mine.wait()

        def finish():
            each_peer(lambda p: send(p, me).wait_send())
            if relay:
                each_peer(lambda p: hand(p, handed).wait_send())

        return start, receive, finish

    x_start, x_receive, x_finish = dispatch(x_send, xr, x_ss, x_rs, xf_ss, xf_rs, load_sem.at[2])
    g_start, g_receive, g_finish = dispatch(g_send, gr, g_ss, g_rs, gf_ss, gf_rs, load_sem.at[3])

    th = tile_of(hidden, 384)
    td = tile_of(width, 256)

    def count_up(shape, axis):
        return lax.broadcasted_iota(jnp.int32, shape, axis).astype(f32)

    down, across = count_up((toks, toks), 0), count_up((toks, toks), 1)
    row_index = count_up((rows, toks), 0)
    col_ids, col_slot = [], []
    for m in range(members):
        row_id = row_ids[m].astype(f32)
        col_id = jnp.sum(jnp.where(down == across, row_id, 0.0), axis=1, keepdims=True)
        same = (col_id == row_id).astype(f32)
        row_slot = jnp.sum(jnp.where(down < across, same, 0.0), axis=0, keepdims=True)
        col_slot.append(jnp.sum(jnp.where(across < down, same, 0.0), axis=1, keepdims=True))
        col_ids.append(col_id)
        row_place = (row_id * members + m) * cap + row_slot
        picks[m] = (row_index == row_place).astype(f32).astype(bf)

    def pack_tokens(j):
        cols = pl.ds(pl.multiple_of(j * td, 128), td)
        value = sum(dot(picks[m], tokens[:, cols], 1, 0) for m in range(members))
        x_send[:, :, cols] = value.astype(bf).reshape(peers, cap, td)

    loop(width // td, pack_tokens)
    pl.semaphore_wait(barrier, peers + zn - 2)
    x_start()

    hot_index = count_up((toks, experts), 1)
    tokens_f = tokens[...].astype(f32)
    for m in range(members):
        hot = (hot_index == col_ids[m]).astype(f32)
        picked_router[m] = dot(hot, router_t[m], 1, 0, lax.Precision.HIGHEST)
        logit = jnp.sum(tokens_f * picked_router[m], axis=-1, keepdims=True)
        gates[m] = 1.0 / (1.0 + jnp.exp(-logit))

    def pack_grads(j):
        cols = pl.ds(pl.multiple_of(j * td, 128), td)
        value = sum(
            dot(picks[m], (gates[m] * out_grad[m, :, cols].astype(f32)).astype(bf), 1, 0)
            for m in range(members)
        )
        g_send[:, :, cols] = value.astype(bf).reshape(peers, cap, td)

    loop(width // td, pack_grads)
    g_start()
    place_index = count_up((toks, dp * cap), 1)
    for m in range(members):
        unperm[m] = (place_index == col_ids[m] * cap + col_slot[m]).astype(f32).astype(bf)

    load1.wait()
    x_receive()

    def first_layer(j):
        cols = pl.ds(pl.multiple_of(j * th, 128), th)
        value, grad = gelu_pair(dot(xr[...].reshape(rows, width), w1[:, cols], 1, 0))
        act[:, cols] = value.astype(bf)
        slope[:, cols] = grad

    loop(hidden // th, first_layer)
    load2.wait()

    by_member = lambda d: (d % members) * dp + d // members

    def give_back(source, target, send_sem, recv_sem, h, own_sem):
        def send(peer, sender):
            return remote(
                source.at[h, peer],
                target.at[h, by_member(sender)],
                send_sem.at[h, peer],
                recv_sem.at[h, sender],
                plane(peer),
            )

        mine = pltpu.make_async_copy(source.at[h, me], target.at[h, by_member(me)], own_sem)

        def start():
            each_peer(lambda p: send(p, me).start())
            mine.start()

        def receive():
            each_peer(lambda p: send(p, p).wait_recv())
            mine.wait()

        return start, receive, lambda: each_peer(lambda p: send(p, me).wait_send())

    outs = [give_back(po, ro, o_ss, o_rs, h, load_sem.at[4 + h]) for h in range(2)]
    dxs = [give_back(pd, rd, d_ss, d_rs, h, load_sem.at[6 + h]) for h in range(2)]

    for h in range(2):
        part = dot(act[...], w2[:, h * half : (h + 1) * half], 1, 0).astype(bf)
        po[h] = part.reshape(peers, cap, half)
        outs[h][0]()

    g_receive()

    def hidden_grad(j):
        cols = pl.ds(pl.multiple_of(j * th, 128), th)
        value = dot(gr[...].reshape(rows, width), w2[cols, :], 1, 1) * slope[:, cols]
        pg[:, cols] = value.astype(bf)

    loop(hidden // th, hidden_grad)
    for h in range(2):
        part = dot(pg[...], w1[h * half : (h + 1) * half, :], 1, 1).astype(bf)
        pd[h] = part.reshape(peers, cap, half)
        dxs[h][0]()

    mid = zn // 2 - 1
    left = me_z < zn // 2
    pos = jnp.where(left, me_z, zn - 1 - me_z)
    inner = jnp.where(left, me_z + 1, me_z - 1)
    outer = jnp.where(left, me_z - 1, me_z + 1)
    out_chunks = members * toks // chunk
    dx_chunks = toks // chunk
    chunks = 2 * (out_chunks + dx_chunks)
    per_member = toks // chunk
    lag = 2
    store1 = pltpu.make_async_copy(first, first_hbm, load_sem.at[0])
    store2 = pltpu.make_async_copy(second, second_hbm, load_sem.at[1])

    def router_in_copy(to, slot):
        return remote(
            router_part.at[to], router_in.at[slot], ri_ss.at[to], ri_rs.at[slot], plane(to)
        )

    def router_copy(z_to, z_from):
        return remote(
            router_row, router_z.at[z_from], rz_ss.at[z_to], rz_rs.at[z_from], {"expert": z_to}
        )

    def router_plane(to, slot):
        return remote(router_sum, router_all.at[slot], rp_ss.at[to], rp_rs.at[slot], plane(to))

    router_own = pltpu.make_async_copy(router_part.at[me], router_in.at[me], load_sem.at[2])
    router_own_z = pltpu.make_async_copy(router_row, router_z.at[me_z], load_sem.at[3])
    router_mine = pltpu.make_async_copy(router_sum, router_all.at[me], load_sem.at[8])

    def second_grads(j):
        cols = pl.ds(pl.multiple_of(j * th, 128), th)
        second[cols, :] = dot(act[:, cols], gr[...].reshape(rows, width), 0, 0).astype(bf)

    def first_grads(j):
        cols = pl.ds(pl.multiple_of(j * td, 128), td)
        first[cols, :] = dot(xr[:, :, cols].reshape(rows, td), pg[...], 0, 0).astype(bf)

    def take_out(h):
        outs[h][1]()
        for m in range(members):
            part = dot(unperm[m], ro[h, m * dp : (m + 1) * dp].reshape(dp * cap, half), 1, 0)
            base = h * out_chunks + m * per_member
            own[base : base + per_member] = part.astype(bf).reshape(per_member, chunk, half)
            grad = out_grad[m, :, h * half : (h + 1) * half].astype(f32)
            partial = jnp.sum(grad * part, axis=-1, keepdims=True)
            gate_grads[m] = partial if h == 0 else gate_grads[m] + partial

    def send_router():
        total = jnp.zeros((peers, width), f32)
        hot_row = lax.broadcasted_iota(jnp.int32, (members * experts, toks), 0)
        for m in range(members):
            hot = (hot_row == row_ids[m] + m * experts).astype(f32)
            weight = gate_grads[m] * gates[m] * (1.0 - gates[m])
            total += dot(hot, tokens[...].astype(f32) * weight, 1, 0, lax.Precision.HIGHEST)
        for p in range(peers):
            router_part[p] = total[p : p + 1]
        router_own.start()
        each_peer(lambda p: router_in_copy(p, me).start())

    def take_dx(h):
        dxs[h][1]()
        total = sum(
            dot(unperm[m], rd[h, m * dp : (m + 1) * dp].reshape(dp * cap, half), 1, 0)
            for m in range(members)
        )
        base = 2 * out_chunks + h * dx_chunks
        own[base : base + dx_chunks] = total.astype(bf).reshape(dx_chunks, chunk, half)

    def add_router():
        router_own.wait()
        each_peer(lambda p: router_in_copy(p, p).wait_recv())
        router_row[...] = jnp.sum(router_in[...], axis=0)
        router_own_z.start()
        each_z(lambda z: router_copy(z, me_z).start())

    def share_router():
        router_own_z.wait()
        each_z(lambda z: router_copy(z, z).wait_recv())
        router_sum[...] = jnp.sum(router_z[...], axis=0)
        router_mine.start()
        each_peer(lambda p: router_plane(p, me).start())

    def line(source, target, send_sem, recv_sem, k, z_to):
        return remote(source.at[k], target.at[k], send_sem.at[k], recv_sem.at[k], {"expert": z_to})

    loop(hidden // th, second_grads)
    store2.start()

    def step(t):
        ka = t - pos
        kb = t - (2 * mid + lag - pos)

        @pl.when((kb >= 0) & (kb < chunks))
        def _():
            @pl.when(pos == mid)
            def _():
                line(own, xch, xch_ss, xch_rs, kb, inner).wait()
                res[kb] = (own[kb].astype(f32) + xch[kb].astype(f32)).astype(bf)

            if mid > 1:

                @pl.when((pos < mid) & (pos > 0))
                def _():
                    line(res, res, res_ss, res_rs, kb, inner).wait_recv()

            @pl.when(pos > 0)
            def _():
                line(res, res, res_ss, res_rs, kb, outer).start()

        @pl.when(ka == 0)
        def _():
            take_out(0)

        @pl.when(ka == out_chunks)
        def _():
            loop(width // td, first_grads)
            store1.start()
            take_out(1)
            send_router()

        @pl.when(ka == 2 * out_chunks)
        def _():
            take_dx(0)
            add_router()

        @pl.when(ka == 2 * out_chunks + dx_chunks)
        def _():
            take_dx(1)
            share_router()

        @pl.when((ka >= 0) & (ka < chunks))
        def _():
            @pl.when(pos > 0)
            def _():
                line(own, red, red_ss, red_rs, ka, outer).wait_recv()
                own[ka] = (own[ka].astype(f32) + red[ka].astype(f32)).astype(bf)

            @pl.when(pos < mid)
            def _():
                line(own, red, red_ss, red_rs, ka, inner).start()

            @pl.when(pos == mid)
            def _():
                line(own, xch, xch_ss, xch_rs, ka, inner).start()

    loop(chunks + 2 * mid + lag, step)

    def last_arrivals(k):
        @pl.when((pos < mid) & (pos == 0))
        def _():
            line(res, res, res_ss, res_rs, k, inner).wait_recv()

    loop(2 * out_chunks, last_arrivals)
    weights = []
    for m in range(members):
        total = jnp.zeros((toks, 1), f32)
        for h in range(2):
            cols = slice(h * half, (h + 1) * half)
            base = h * out_chunks + m * per_member
            value = res[base : base + per_member].reshape(toks, half).astype(f32)
            moe_out[m, :, cols] = (gates[m] * value).astype(bf)
            grad = out_grad[m, :, cols].astype(f32)
            total += jnp.sum(grad * value, axis=-1, keepdims=True)
        weights.append(total * gates[m] * (1.0 - gates[m]))
    loop(chunks - 2 * out_chunks, lambda k: last_arrivals(k + 2 * out_chunks))
    for h in range(2):
        cols = slice(h * half, (h + 1) * half)
        base = 2 * out_chunks + h * dx_chunks
        value = res[base : base + dx_chunks].reshape(toks, half).astype(f32)
        for m in range(members):
            value += weights[m] * picked_router[m, :, cols]
        token_grad[:, cols] = value

    def drain(k):
        @pl.when(pos < mid)
        def _():
            line(own, red, red_ss, red_rs, k, inner).wait_send()

        @pl.when(pos > 0)
        def _():
            line(res, res, res_ss, res_rs, k, outer).wait_send()

    loop(chunks, drain)
    x_finish()
    g_finish()
    for h in range(2):
        outs[h][2]()
        dxs[h][2]()
    store1.wait()
    store2.wait()
    each_peer(lambda p: router_in_copy(p, me).wait_send())
    each_z(lambda z: router_copy(z, me_z).wait_send())
    each_peer(lambda p: router_plane(p, me).wait_send())
    each_peer(lambda p: router_plane(p, p).wait_recv())
    router_mine.wait()


parts = 8


def write_out(moe, grad, first, second, routers, moe_to, grad_to, first_to, second_to, router_to):
    moe_to[...] = moe[...]
    grad_to[...] = grad[...]
    first_to[...] = first[...]
    second_to[...] = second[...]

    @pl.when(pl.program_id(0) == 0)
    def _():
        members, experts = router_to.shape[:2]
        for m in range(members):
            for e in range(experts):
                router_to[m, e : e + 1] = routers[m * experts + e]


def shards(tokens, route_ids, router, w_in, w_out, out_grad):
    members, toks = route_ids.shape[:2]
    experts, width = router.shape[2], tokens.shape[1]
    dp, zn = lax.axis_size("dp"), lax.axis_size("expert")
    peers = dp * members
    hidden = w_in.shape[3]
    capacity = max(2, 3 * toks // (2 * experts))
    cap = -(-capacity // 16) * 16
    rows = peers * cap
    chunk = toks // 2
    half = width // 2
    bf, f32 = jnp.bfloat16, jnp.float32

    vmem, anywhere = pl.BlockSpec(memory_space=pltpu.VMEM), pl.BlockSpec(memory_space=pl.ANY)
    chunks = 2 * (members + 1) * toks // chunk
    dma = pltpu.SemaphoreType.DMA
    block = pltpu.VMEM((peers, cap, width), bf)
    halves = pltpu.VMEM((2, peers, cap, half), bf)
    line = pltpu.VMEM((chunks, chunk, half), bf)
    moe_out, token_grad, first, second, router_all = pl.pallas_call(
        functools.partial(layer_kernel, (dp, members, zn, cap, toks, chunk)),
        out_shape=(
            jax.ShapeDtypeStruct((members, toks, width), bf),
            jax.ShapeDtypeStruct((toks, width), f32),
            jax.ShapeDtypeStruct((width, hidden), bf),
            jax.ShapeDtypeStruct((hidden, width), bf),
            jax.ShapeDtypeStruct((peers, 1, width), f32),
        ),
        in_specs=[vmem] * 4 + [anywhere] * 2,
        out_specs=(vmem, vmem, anywhere, anywhere, anywhere),
        scratch_shapes=[
            block,
            block,
            pltpu.VMEM((members, rows, toks), bf),
            pltpu.VMEM((members, toks, dp * cap), bf),
            pltpu.VMEM((members, toks, width), f32),
            pltpu.VMEM((members, toks, 1), f32),
            pltpu.VMEM((members, toks, 1), f32),
            pltpu.VMEM((width, hidden), bf),
            pltpu.VMEM((hidden, width), bf),
            block,
            block,
            pltpu.VMEM((rows, hidden), bf),
            pltpu.VMEM((rows, hidden), f32),
            pltpu.VMEM((rows, hidden), bf),
            halves,
            halves,
            halves,
            halves,
            pltpu.VMEM((width, hidden), bf),
            pltpu.VMEM((hidden, width), bf),
            line,
            line,
            line,
            line,
            pltpu.VMEM((peers, 1, width), f32),
            pltpu.VMEM((peers, 1, width), f32),
            pltpu.VMEM((1, width), f32),
            pltpu.VMEM((zn, 1, width), f32),
            pltpu.VMEM((1, width), f32),
            dma((9,)),
        ]
        + [dma((peers,))] * 8
        + [dma((2, peers))] * 4
        + [dma((chunks,))] * 6
        + [dma((zn,))] * 2
        + [dma((peers,))] * 4,
        compiler_params=pltpu.CompilerParams(
            collective_id=0, has_side_effects=True, vmem_limit_bytes=60 * 1024 * 1024
        ),
        cost_estimate=pl.CostEstimate(
            flops=12 * rows * width * hidden,
            bytes_accessed=8 * width * hidden,
            transcendentals=rows * hidden,
        ),
    )(
        jnp.swapaxes(route_ids, 1, 2),
        tokens,
        out_grad,
        jnp.swapaxes(router, 1, 2),
        w_in[0, 0],
        w_out[0, 0],
    )
    finals = (moe_out, token_grad, first, second)
    pieces = [
        pl.BlockSpec((members, toks // parts, width), lambda i: (0, i, 0)),
        pl.BlockSpec((toks // parts, width), lambda i: (i, 0)),
        pl.BlockSpec((width // parts, hidden), lambda i: (i, 0)),
        pl.BlockSpec((hidden // parts, width), lambda i: (i, 0)),
    ]
    moe_out, token_grad, first, second, router_sum = pl.pallas_call(
        write_out,
        grid=(parts,),
        out_shape=tuple(jax.ShapeDtypeStruct(v.shape, v.dtype) for v in finals)
        + (jax.ShapeDtypeStruct((members, experts, width), f32),),
        in_specs=pieces + [pl.BlockSpec(router_all.shape, lambda i: (0, 0, 0))],
        out_specs=tuple(pieces) + (pl.BlockSpec((members, experts, width), lambda i: (0, 0, 0)),),
        compiler_params=pltpu.CompilerParams(vmem_limit_bytes=60 * 1024 * 1024),
    )(*finals, router_all)
    router_grad = jnp.swapaxes(router_sum, 1, 2)
    return (moe_out, token_grad, first[None, None], second[None, None], router_grad)


def solution(mesh):
    in_specs = (
        P(("dp", "member"), None),
        P(None, ("dp", "member"), None),
        P(),
        P("member", "dp", None, "expert"),
        P("member", "dp", "expert", None),
        P(None, ("dp", "member"), None),
    )
    out_specs = (
        P(None, ("dp", "member"), None),
        P(("dp", "member"), None),
        P("member", "dp", None, "expert"),
        P("member", "dp", "expert", None),
        P(),
    )
    return jax.shard_map(shards, mesh=mesh, in_specs=in_specs, out_specs=out_specs, check_vma=False)
```

```python
import functools

import jax
import jax.numpy as jnp
from jax import lax
from jax.experimental import pallas as pl
from jax.experimental.pallas import tpu as pltpu
from jax.sharding import PartitionSpec as P

MESH = pl.DeviceIdType.MESH
tanh_scale = 0.7978845608028654
cubic_term = 0.044715


def gelu_pair(pre_act):
    square = pre_act * pre_act
    tanh_value = jnp.tanh(tanh_scale * (pre_act + cubic_term * square * pre_act))
    half = 0.5 * (1.0 + tanh_value)
    slope = half + 0.5 * pre_act * (1.0 - tanh_value * tanh_value) * tanh_scale * (
        1.0 + 3.0 * cubic_term * square
    )
    return pre_act * half, slope


def dot(a, b, ca, cb, precision=None):
    return lax.dot_general(
        a, b, (((ca,), (cb,)), ((), ())), precision=precision, preferred_element_type=jnp.float32
    )


def tile_of(size, wanted):
    while size % wanted:
        wanted -= 128
    return wanted


def layer_kernel(
    cfg,
    row_ids, tokens, out_grad, router_t, w1_hbm, w2_hbm,
    moe_out, token_grad, first_hbm, second_hbm, router_all,
    x_send, g_send, picks, unperm, picked_router, gates, gate_grads,
    w1, w2, xr, gr, act, slope, pg, po, pd, ro, rd, first, second,
    own, red, xch, res, router_part, router_in, router_row, router_z, router_sum,
    load_sem, x_ss, x_rs, g_ss, g_rs, xf_ss, xf_rs, gf_ss, gf_rs, o_ss, o_rs, d_ss, d_rs,
    red_ss, red_rs, xch_ss, xch_rs, res_ss, res_rs, rz_ss, rz_rs, rp_ss, rp_rs, ri_ss, ri_rs,
):
    dp, members, zn, cap, toks, chunk = cfg
    peers = dp * members
    me_dp, me_m, me_z = lax.axis_index("dp"), lax.axis_index("member"), lax.axis_index("expert")
    me = me_dp * members + me_m
    width = x_send.shape[-1]
    half = width // 2
    hidden = w1.shape[1]
    rows = peers * cap
    experts = router_t.shape[1]
    bf, f32 = jnp.bfloat16, jnp.float32

    def plane(index):
        return {"dp": index // members, "member": index % members}

    def loop(count, body):
        lax.fori_loop(0, count, lambda i, c: (body(i), c)[1], 0)

    def each_peer(body):
        loop(peers - 1, lambda i: body((me + 1 + (i + (peers - 2) * me_m) % (peers - 1)) % peers))

    def each_z(body):
        loop(zn - 1, lambda i: body((me_z + 1 + i) % zn))

    def remote(source, target, send_sem, recv_sem, where):
        return pltpu.make_async_remote_copy(
            src_ref=source,
            dst_ref=target,
            send_sem=send_sem,
            recv_sem=recv_sem,
            device_id=where,
            device_id_type=MESH,
        )

    barrier = pltpu.get_barrier_semaphore()
    each_peer(
        lambda p: pl.semaphore_signal(barrier, inc=1, device_id=plane(p), device_id_type=MESH)
    )
    each_z(
        lambda z: pl.semaphore_signal(barrier, inc=1, device_id={"expert": z}, device_id_type=MESH)
    )
    load1 = pltpu.make_async_copy(w1_hbm, w1, load_sem.at[0])
    load2 = pltpu.make_async_copy(w2_hbm, w2, load_sem.at[1])
    load1.start()
    load2.start()

    relay = cap % 48 == 0
    third = cap // 3
    parity = me_z % 2
    partner = me_z + 1 - 2 * parity
    if relay:
        sent = pl.ds(pl.multiple_of(parity * third, 16), 2 * third)
        handed = pl.ds(pl.multiple_of(parity * 2 * third, 16), third)
        taken = pl.ds(pl.multiple_of((1 - parity) * 2 * third, 16), third)
    else:
        sent = pl.ds(0, cap)

    def dispatch(source, target, send_sem, recv_sem, relay_ss, relay_rs, own_sem):
        def send(peer, slot):
            return remote(
                source.at[peer, sent], target.at[slot, sent], send_sem.at[peer], recv_sem.at[slot], plane(peer)
            )

        def hand(peer, part):
            return remote(
                target.at[peer, part],
                target.at[peer, part],
                relay_ss.at[peer],
                relay_rs.at[peer],
                {"expert": partner},
            )

        mine = pltpu.make_async_copy(source.at[me], target.at[me], own_sem)

        def start():
            each_peer(lambda p: send(p, me).start())
            mine.start()

        def receive():
            def one(p):
                send(p, p).wait_recv()
                if relay:
                    hand(p, handed).start()

            each_peer(one)
            if relay:
                each_peer(lambda p: hand(p, taken).wait_recv())
            mine.wait()

        def finish():
            each_peer(lambda p: send(p, me).wait_send())
            if relay:
                each_peer(lambda p: hand(p, handed).wait_send())

        return start, receive, finish

    x_start, x_receive, x_finish = dispatch(x_send, xr, x_ss, x_rs, xf_ss, xf_rs, load_sem.at[2])
    g_start, g_receive, g_finish = dispatch(g_send, gr, g_ss, g_rs, gf_ss, gf_rs, load_sem.at[3])

    th = tile_of(hidden, 384)
    td = tile_of(width, 256)

    def count_up(shape, axis):
        return lax.broadcasted_iota(jnp.int32, shape, axis).astype(f32)

    down, across = count_up((toks, toks), 0), count_up((toks, toks), 1)
    row_index = count_up((rows, toks), 0)
    col_ids, col_slot = [], []
    for m in range(members):
        row_id = row_ids[m].astype(f32)
        col_id = jnp.sum(jnp.where(down == across, row_id, 0.0), axis=1, keepdims=True)
        same = (col_id == row_id).astype(f32)
        row_slot = jnp.sum(jnp.where(down < across, same, 0.0), axis=0, keepdims=True)
        col_slot.append(jnp.sum(jnp.where(across < down, same, 0.0), axis=1, keepdims=True))
        col_ids.append(col_id)
        row_place = (row_id * members + m) * cap + row_slot
        picks[m] = (row_index == row_place).astype(f32).astype(bf)

    def pack_tokens(j):
        cols = pl.ds(pl.multiple_of(j * td, 128), td)
        value = sum(dot(picks[m], tokens[:, cols], 1, 0) for m in range(members))
        x_send[:, :, cols] = value.astype(bf).reshape(peers, cap, td)

    loop(width // td, pack_tokens)
    pl.semaphore_wait(barrier, peers + zn - 2)
    x_start()

    hot_index = count_up((toks, experts), 1)
    tokens_f = tokens[...].astype(f32)
    for m in range(members):
        hot = (hot_index == col_ids[m]).astype(f32)
        picked_router[m] = dot(hot, router_t[m], 1, 0, lax.Precision.HIGHEST)
        logit = jnp.sum(tokens_f * picked_router[m], axis=-1, keepdims=True)
        gates[m] = 1.0 / (1.0 + jnp.exp(-logit))

    def pack_grads(j):
        cols = pl.ds(pl.multiple_of(j * td, 128), td)
        value = sum(
            dot(picks[m], (gates[m] * out_grad[m, :, cols].astype(f32)).astype(bf), 1, 0)
            for m in range(members)
        )
        g_send[:, :, cols] = value.astype(bf).reshape(peers, cap, td)

    loop(width // td, pack_grads)
    g_start()
    place_index = count_up((toks, dp * cap), 1)
    for m in range(members):
        unperm[m] = (place_index == col_ids[m] * cap + col_slot[m]).astype(f32).astype(bf)

    load1.wait()
    x_receive()

    def first_layer(j):
        cols = pl.ds(pl.multiple_of(j * th, 128), th)
        value, grad = gelu_pair(dot(xr[...].reshape(rows, width), w1[:, cols], 1, 0))
        act[:, cols] = value.astype(bf)
        slope[:, cols] = grad

    loop(hidden // th, first_layer)
    load2.wait()

    by_member = lambda d: (d % members) * dp + d // members

    def give_back(source, target, send_sem, recv_sem, h, own_sem):
        def send(peer, sender):
            return remote(
                source.at[h, peer],
                target.at[h, by_member(sender)],
                send_sem.at[h, peer],
                recv_sem.at[h, sender],
                plane(peer),
            )

        mine = pltpu.make_async_copy(source.at[h, me], target.at[h, by_member(me)], own_sem)

        def start():
            each_peer(lambda p: send(p, me).start())
            mine.start()

        def receive():
            each_peer(lambda p: send(p, p).wait_recv())
            mine.wait()

        return start, receive, lambda: each_peer(lambda p: send(p, me).wait_send())

    outs = [give_back(po, ro, o_ss, o_rs, h, load_sem.at[4 + h]) for h in range(2)]
    dxs = [give_back(pd, rd, d_ss, d_rs, h, load_sem.at[6 + h]) for h in range(2)]

    for h in range(2):
        part = dot(act[...], w2[:, h * half : (h + 1) * half], 1, 0).astype(bf)
        po[h] = part.reshape(peers, cap, half)
        outs[h][0]()

    g_receive()

    def hidden_grad(j):
        cols = pl.ds(pl.multiple_of(j * th, 128), th)
        value = dot(gr[...].reshape(rows, width), w2[cols, :], 1, 1) * slope[:, cols]
        pg[:, cols] = value.astype(bf)

    loop(hidden // th, hidden_grad)
    for h in range(2):
        part = dot(pg[...], w1[h * half : (h + 1) * half, :], 1, 1).astype(bf)
        pd[h] = part.reshape(peers, cap, half)
        dxs[h][0]()

    mid = zn // 2 - 1
    left = me_z < zn // 2
    pos = jnp.where(left, me_z, zn - 1 - me_z)
    inner = jnp.where(left, me_z + 1, me_z - 1)
    outer = jnp.where(left, me_z - 1, me_z + 1)
    out_chunks = members * toks // chunk
    dx_chunks = toks // chunk
    chunks = 2 * (out_chunks + dx_chunks)
    per_member = toks // chunk
    lag = 2
    store1 = pltpu.make_async_copy(first, first_hbm, load_sem.at[0])
    store2 = pltpu.make_async_copy(second, second_hbm, load_sem.at[1])

    def router_in_copy(to, slot):
        return remote(
            router_part.at[to], router_in.at[slot], ri_ss.at[to], ri_rs.at[slot], plane(to)
        )

    def router_copy(z_to, z_from):
        return remote(
            router_row, router_z.at[z_from], rz_ss.at[z_to], rz_rs.at[z_from], {"expert": z_to}
        )

    def router_plane(to, slot):
        return remote(router_sum, router_all.at[slot], rp_ss.at[to], rp_rs.at[slot], plane(to))

    router_own = pltpu.make_async_copy(router_part.at[me], router_in.at[me], load_sem.at[2])
    router_own_z = pltpu.make_async_copy(router_row, router_z.at[me_z], load_sem.at[3])
    router_mine = pltpu.make_async_copy(router_sum, router_all.at[me], load_sem.at[8])

    def second_grads(j):
        cols = pl.ds(pl.multiple_of(j * th, 128), th)
        second[cols, :] = dot(act[:, cols], gr[...].reshape(rows, width), 0, 0).astype(bf)

    def first_grads(j):
        cols = pl.ds(pl.multiple_of(j * td, 128), td)
        first[cols, :] = dot(xr[:, :, cols].reshape(rows, td), pg[...], 0, 0).astype(bf)

    def take_out(h):
        outs[h][1]()
        for m in range(members):
            part = dot(unperm[m], ro[h, m * dp : (m + 1) * dp].reshape(dp * cap, half), 1, 0)
            base = h * out_chunks + m * per_member
            own[base : base + per_member] = part.astype(bf).reshape(per_member, chunk, half)
            grad = out_grad[m, :, h * half : (h + 1) * half].astype(f32)
            partial = jnp.sum(grad * part, axis=-1, keepdims=True)
            gate_grads[m] = partial if h == 0 else gate_grads[m] + partial

    def send_router():
        total = jnp.zeros((peers, width), f32)
        hot_row = lax.broadcasted_iota(jnp.int32, (members * experts, toks), 0)
        for m in range(members):
            hot = (hot_row == row_ids[m] + m * experts).astype(f32)
            weight = gate_grads[m] * gates[m] * (1.0 - gates[m])
            total += dot(hot, tokens[...].astype(f32) * weight, 1, 0, lax.Precision.HIGHEST)
        for p in range(peers):
            router_part[p] = total[p : p + 1]
        router_own.start()
        each_peer(lambda p: router_in_copy(p, me).start())

    def take_dx(h):
        dxs[h][1]()
        total = sum(
            dot(unperm[m], rd[h, m * dp : (m + 1) * dp].reshape(dp * cap, half), 1, 0)
            for m in range(members)
        )
        base = 2 * out_chunks + h * dx_chunks
        own[base : base + dx_chunks] = total.astype(bf).reshape(dx_chunks, chunk, half)

    def add_router():
        router_own.wait()
        each_peer(lambda p: router_in_copy(p, p).wait_recv())
        router_row[...] = jnp.sum(router_in[...], axis=0)
        router_own_z.start()
        each_z(lambda z: router_copy(z, me_z).start())

    def share_router():
        router_own_z.wait()
        each_z(lambda z: router_copy(z, z).wait_recv())
        router_sum[...] = jnp.sum(router_z[...], axis=0)
        router_mine.start()
        each_peer(lambda p: router_plane(p, me).start())

    def line(source, target, send_sem, recv_sem, k, z_to):
        return remote(source.at[k], target.at[k], send_sem.at[k], recv_sem.at[k], {"expert": z_to})

    loop(hidden // th, second_grads)
    store2.start()

    def step(t):
        ka = t - pos
        kb = t - (2 * mid + lag - pos)

        @pl.when((kb >= 0) & (kb < chunks))
        def _():
            @pl.when(pos == mid)
            def _():
                line(own, xch, xch_ss, xch_rs, kb, inner).wait()
                res[kb] = (own[kb].astype(f32) + xch[kb].astype(f32)).astype(bf)

            if mid > 1:

                @pl.when((pos < mid) & (pos > 0))
                def _():
                    line(res, res, res_ss, res_rs, kb, inner).wait_recv()

            @pl.when(pos > 0)
            def _():
                line(res, res, res_ss, res_rs, kb, outer).start()

        @pl.when(ka == 0)
        def _():
            take_out(0)

        @pl.when(ka == out_chunks)
        def _():
            loop(width // td, first_grads)
            store1.start()
            take_out(1)
            send_router()

        @pl.when(ka == 2 * out_chunks)
        def _():
            take_dx(0)
            add_router()

        @pl.when(ka == 2 * out_chunks + dx_chunks)
        def _():
            take_dx(1)
            share_router()

        @pl.when((ka >= 0) & (ka < chunks))
        def _():
            @pl.when(pos > 0)
            def _():
                line(own, red, red_ss, red_rs, ka, outer).wait_recv()
                own[ka] = (own[ka].astype(f32) + red[ka].astype(f32)).astype(bf)

            @pl.when(pos < mid)
            def _():
                line(own, red, red_ss, red_rs, ka, inner).start()

            @pl.when(pos == mid)
            def _():
                line(own, xch, xch_ss, xch_rs, ka, inner).start()

    loop(chunks + 2 * mid + lag, step)

    def last_arrivals(k):
        @pl.when((pos < mid) & (pos == 0))
        def _():
            line(res, res, res_ss, res_rs, k, inner).wait_recv()

    loop(2 * out_chunks, last_arrivals)
    weights = []
    for m in range(members):
        total = jnp.zeros((toks, 1), f32)
        for h in range(2):
            cols = slice(h * half, (h + 1) * half)
            base = h * out_chunks + m * per_member
            value = res[base : base + per_member].reshape(toks, half).astype(f32)
            moe_out[m, :, cols] = (gates[m] * value).astype(bf)
            grad = out_grad[m, :, cols].astype(f32)
            total += jnp.sum(grad * value, axis=-1, keepdims=True)
        weights.append(total * gates[m] * (1.0 - gates[m]))
    loop(chunks - 2 * out_chunks, lambda k: last_arrivals(k + 2 * out_chunks))
    for h in range(2):
        cols = slice(h * half, (h + 1) * half)
        base = 2 * out_chunks + h * dx_chunks
        value = res[base : base + dx_chunks].reshape(toks, half).astype(f32)
        for m in range(members):
            value += weights[m] * picked_router[m, :, cols]
        token_grad[:, cols] = value

    def drain(k):
        @pl.when(pos < mid)
        def _():
            line(own, red, red_ss, red_rs, k, inner).wait_send()

        @pl.when(pos > 0)
        def _():
            line(res, res, res_ss, res_rs, k, outer).wait_send()

    loop(chunks, drain)
    x_finish()
    g_finish()
    for h in range(2):
        outs[h][2]()
        dxs[h][2]()
    store1.wait()
    store2.wait()
    each_peer(lambda p: router_in_copy(p, me).wait_send())
    each_z(lambda z: router_copy(z, me_z).wait_send())
    each_peer(lambda p: router_plane(p, me).wait_send())
    each_peer(lambda p: router_plane(p, p).wait_recv())
    router_mine.wait()


parts = 4


def write_out(
    first, second, moe, grad, routers, first_to, second_to, moe_to, grad_to, router_to,
    first_held, second_held, moe_held, grad_held, in_sem, out_sem,
):
    trips = []
    for source, held, target, count in (
        (first, first_held, first_to, parts),
        (second, second_held, second_to, parts),
        (moe, moe_held, moe_to, 1),
        (grad, grad_held, grad_to, 1),
    ):
        size = source.shape[0] // count
        for k in range(count):
            piece, slot = pl.ds(k * size, size), len(trips)
            trips.append(
                (
                    pltpu.make_async_copy(source.at[piece], held.at[piece], in_sem.at[slot]),
                    pltpu.make_async_copy(held.at[piece], target.at[piece], out_sem.at[slot]),
                )
            )
    for fetch, _ in trips:
        fetch.start()
    members, experts = router_to.shape[:2]
    for m in range(members):
        for e in range(experts):
            router_to[m, e : e + 1] = routers[m * experts + e]
    for fetch, put in trips:
        fetch.wait()
        put.start()
    for _, put in trips:
        put.wait()


def shards(tokens, route_ids, router, w_in, w_out, out_grad):
    members, toks = route_ids.shape[:2]
    experts, width = router.shape[2], tokens.shape[1]
    dp, zn = lax.axis_size("dp"), lax.axis_size("expert")
    peers = dp * members
    hidden = w_in.shape[3]
    capacity = max(2, 3 * toks // (2 * experts))
    cap = -(-capacity // 16) * 16
    rows = peers * cap
    chunk = toks // 2
    half = width // 2
    bf, f32 = jnp.bfloat16, jnp.float32

    vmem, anywhere = pl.BlockSpec(memory_space=pltpu.VMEM), pl.BlockSpec(memory_space=pl.ANY)
    chunks = 2 * (members + 1) * toks // chunk
    dma = pltpu.SemaphoreType.DMA
    block = pltpu.VMEM((peers, cap, width), bf)
    halves = pltpu.VMEM((2, peers, cap, half), bf)
    line = pltpu.VMEM((chunks, chunk, half), bf)
    moe_out, token_grad, first, second, router_all = pl.pallas_call(
        functools.partial(layer_kernel, (dp, members, zn, cap, toks, chunk)),
        out_shape=(
            jax.ShapeDtypeStruct((members, toks, width), bf),
            jax.ShapeDtypeStruct((toks, width), f32),
            jax.ShapeDtypeStruct((width, hidden), bf),
            jax.ShapeDtypeStruct((hidden, width), bf),
            jax.ShapeDtypeStruct((peers, 1, width), f32),
        ),
        in_specs=[vmem] * 4 + [anywhere] * 2,
        out_specs=(vmem, vmem, anywhere, anywhere, anywhere),
        scratch_shapes=[
            block,
            block,
            pltpu.VMEM((members, rows, toks), bf),
            pltpu.VMEM((members, toks, dp * cap), bf),
            pltpu.VMEM((members, toks, width), f32),
            pltpu.VMEM((members, toks, 1), f32),
            pltpu.VMEM((members, toks, 1), f32),
            pltpu.VMEM((width, hidden), bf),
            pltpu.VMEM((hidden, width), bf),
            block,
            block,
            pltpu.VMEM((rows, hidden), bf),
            pltpu.VMEM((rows, hidden), f32),
            pltpu.VMEM((rows, hidden), bf),
            halves,
            halves,
            halves,
            halves,
            pltpu.VMEM((width, hidden), bf),
            pltpu.VMEM((hidden, width), bf),
            line,
            line,
            line,
            line,
            pltpu.VMEM((peers, 1, width), f32),
            pltpu.VMEM((peers, 1, width), f32),
            pltpu.VMEM((1, width), f32),
            pltpu.VMEM((zn, 1, width), f32),
            pltpu.VMEM((1, width), f32),
            dma((9,)),
        ]
        + [dma((peers,))] * 8
        + [dma((2, peers))] * 4
        + [dma((chunks,))] * 6
        + [dma((zn,))] * 2
        + [dma((peers,))] * 4,
        compiler_params=pltpu.CompilerParams(
            collective_id=0, has_side_effects=True, vmem_limit_bytes=60 * 1024 * 1024
        ),
        cost_estimate=pl.CostEstimate(
            flops=12 * rows * width * hidden,
            bytes_accessed=8 * width * hidden,
            transcendentals=rows * hidden,
        ),
    )(
        jnp.swapaxes(route_ids, 1, 2),
        tokens,
        out_grad,
        jnp.swapaxes(router, 1, 2),
        w_in[0, 0],
        w_out[0, 0],
    )
    finals = (first, second, moe_out, token_grad)
    first, second, moe_out, token_grad, router_sum = pl.pallas_call(
        write_out,
        out_shape=tuple(jax.ShapeDtypeStruct(v.shape, v.dtype) for v in finals)
        + (jax.ShapeDtypeStruct((members, experts, width), f32),),
        in_specs=[anywhere] * 4 + [vmem],
        out_specs=(anywhere,) * 4 + (vmem,),
        scratch_shapes=[pltpu.VMEM(v.shape, v.dtype) for v in finals]
        + [dma((2 * parts + 2,))] * 2,
        compiler_params=pltpu.CompilerParams(vmem_limit_bytes=60 * 1024 * 1024),
    )(*finals, router_all)
    router_grad = jnp.swapaxes(router_sum, 1, 2)
    return (moe_out, token_grad, first[None, None], second[None, None], router_grad)


def solution(mesh):
    in_specs = (
        P(("dp", "member"), None),
        P(None, ("dp", "member"), None),
        P(),
        P("member", "dp", None, "expert"),
        P("member", "dp", "expert", None),
        P(None, ("dp", "member"), None),
    )
    out_specs = (
        P(None, ("dp", "member"), None),
        P(("dp", "member"), None),
        P("member", "dp", None, "expert"),
        P("member", "dp", "expert", None),
        P(),
    )
    return jax.shard_map(shards, mesh=mesh, in_specs=in_specs, out_specs=out_specs, check_vma=False)
```
